128 devices in a mesh: tm: 4 (over z_hi, core), space: 32 (over z_lo, y, x).
Axes of the slice: x: 4, y: 4, z: 4 (z_hi: 2, z_lo: 2; z = z_hi * 2 + z_lo), core: 2. Of those that a mesh axis runs over, the one named last changes fastest.
Arguments:
- start_states: float32 [4, 2, 384, 256, 256], P('tm', None, 'space'), may hold values from -6 to 6
- velocity: float32 [3, 384, 256, 256], P(None, 'space'), may hold values from -0.1 to 0.1
- site_class: int32 [384, 256, 256], P('space'), may hold values from 0 to 7
- attach_rates: float32 [8], replicated, may hold values from 0.01 to 0.2
- detach_rates: float32 [8], replicated, may hold values from 0.005 to 0.1
Outputs:
- new_states: float32 [4, 2, 384, 256, 256], P('tm', None, 'space')
The draws below stay inside these ranges and needn't reach their ends.
All inputs are finite; a program needn't handle non-finite values.
Results may differ from the reference program's by a relative error of at most 0.0001.
Values sent between devices are 32-bit elements; how exact they have to be, the bound alone decides.
A program may use at most 192 MiB of HBM per device.

```python
import math
import jax
import jax.numpy as jnp
from jax import lax

NY = 256
NZ = 256
FSTEPS = 4
CSTEPS = 2
KCLS = 8
NX = 384
N_TM = 4


def with_ends(values, rng, smallest, largest):
    shape = values.shape
    place = [jax.random.randint(jax.random.fold_in(rng, axis), (), 0, shape[axis]) for axis in range(len(shape))]
    values = values.at[tuple(place)].set(smallest)
    longest = shape.index(max(shape))
    place[longest] = (place[longest] + 1) % shape[longest]
    return values.at[tuple(place)].set(largest)


def level_of(stream_key, extent, cuts, least, largest):
    def one(dim, shards_of):
        steps = jax.random.uniform(jax.random.fold_in(jax.random.fold_in(stream_key, 6), dim), (shards_of,), jnp.float32, least / len(cuts), largest / len(cuts))
        return jnp.repeat(jnp.exp(steps), extent[dim] // shards_of).reshape((-1,) + (1,) * (len(extent) - dim - 1))

    level = one(*cuts[0])
    for cut in cuts[1:]:
        level = level * one(*cut)
    return level


def normal_values(own_key, shape, scale, reach, cuts=(), kind=jnp.bfloat16):
    level = level_of(own_key, shape, cuts, -0.22, 0.18) if cuts else 1.0
    entries = jax.random.normal(own_key, shape, jnp.float32) * scale * level
    return jnp.minimum(jnp.maximum(entries, -reach), reach).astype(kind)


def setup_inputs(seed: int = 0) -> dict:
    streams_of = jax.random.split(jax.random.key(seed), 6)
    return {
        "start_states": normal_values(streams_of[0], (N_TM, 2, NX, NY, NZ), 1.0, 6.0, ((0, 4), (2, 32)), jnp.float32),
        "velocity": jnp.clip(jax.random.uniform(streams_of[1], (3, NX, NY, NZ), jnp.float32, -0.1, 0.1) * level_of(streams_of[1], (3, NX, NY, NZ), ((1, 32),), -0.4, 0.0), -0.1, 0.1),
        "site_class": with_ends(jax.random.randint(streams_of[2], (NX, NY, NZ), 0, KCLS), jax.random.fold_in(streams_of[2], 1), 0, KCLS - 1).astype(jnp.int32),
        "attach_rates": jnp.clip(jnp.exp(jax.random.uniform(streams_of[3], (KCLS,), jnp.float32, math.log(0.01), math.log(0.2))), 0.01, 0.2),
        "detach_rates": jnp.clip(jnp.exp(jax.random.uniform(streams_of[4], (KCLS,), jnp.float32, math.log(0.005), math.log(0.1))), 0.005, 0.1),
    }


dispersion = 0.08


def restrict(values):
    leading = values.shape[:-3]
    extra = len(leading)
    blocks = values.reshape(leading + (values.shape[-3] // 2, 2, values.shape[-2] // 2, 2, values.shape[-1] // 2, 2))
    return jnp.mean(blocks, axis=(extra + 1, extra + 3, extra + 5))


def prolong(values):
    return jnp.repeat(jnp.repeat(jnp.repeat(values, 2, axis=-3), 2, axis=-2), 2, axis=-1)


def shift_zero(values, axis, by):
    padding = [(0, 0)] * values.ndim
    padding[axis] = (1, 0) if by > 0 else (0, 1)
    padded = jnp.pad(values, padding)
    length = values.shape[axis]
    offset = 0 if by > 0 else 1
    return lax.slice_in_dim(padded, offset, offset + length, axis=axis)


def class_rates(site_class, rate_table):
    summed = jnp.zeros(site_class.shape, rate_table.dtype)
    for level in range(rate_table.shape[0]):
        summed = summed + jnp.where(site_class == level, rate_table[level], 0.0)
    return summed


def coefficients(velocity, rim, spread):
    plus_first = jnp.maximum(rim, 0.0) + spread
    minus_first = jnp.maximum(-rim, 0.0) + spread
    plus_second = jnp.maximum(velocity[1], 0.0) + spread
    minus_second = jnp.maximum(-velocity[1], 0.0) + spread
    plus_third = jnp.maximum(velocity[2], 0.0) + spread
    minus_third = jnp.maximum(-velocity[2], 0.0) + spread
    outflow = jnp.abs(velocity[0]) + jnp.abs(velocity[1]) + jnp.abs(velocity[2]) + 6.0 * spread
    return (plus_first, minus_first, plus_second, minus_second, plus_third, minus_third, outflow)


def advance(mobile, attached, coefs, attach_rate, detach_rate, exchange):
    plus_first, minus_first, plus_second, minus_second, plus_third, minus_third, outflow = coefs
    padded = exchange(mobile)
    flow_first = plus_first[:-2] * padded[:-2] + minus_first[2:] * padded[2:]
    flow_second = shift_zero(plus_second * mobile, 1, 1) + shift_zero(minus_second * mobile, 1, -1)
    flow_third = shift_zero(plus_third * mobile, 2, 1) + shift_zero(minus_third * mobile, 2, -1)
    inflow = flow_first + flow_second + flow_third
    exchanged = attach_rate * mobile - detach_rate * attached
    return mobile + inflow - outflow * mobile - exchanged, attached + exchanged


def pad_first(values):
    return jnp.pad(values, ((1, 1), (0, 0), (0, 0)))


def reference(start_states, velocity, site_class, attach_rates, detach_rates):
    attach_rate = class_rates(site_class, attach_rates)
    detach_rate = class_rates(site_class, detach_rates)
    wide_rim = jnp.pad(velocity[0], ((2, 2), (0, 0), (0, 0)))
    fine_coefs = coefficients(velocity, wide_rim[1:-1], dispersion)
    coarse_coefs = coefficients(restrict(velocity), restrict(wide_rim), 0.5 * dispersion)
    coarse_attach = 2.0 * restrict(attach_rate)
    coarse_detach = 2.0 * restrict(detach_rate)

    def propagate(coarse_pair):
        mobile, attached = coarse_pair[0], coarse_pair[1]
        for turn in range(CSTEPS):
            mobile, attached = advance(mobile, attached, coarse_coefs, coarse_attach, coarse_detach, pad_first)
        return jnp.stack([mobile, attached])

    slice_ends = []
    for slice_number in range(N_TM):
        mobile, attached = start_states[slice_number, 0], start_states[slice_number, 1]
        for turn in range(FSTEPS):
            mobile, attached = advance(mobile, attached, fine_coefs, attach_rate, detach_rate, pad_first)
        slice_ends.append(jnp.stack([mobile, attached]))
    coarse_prev = jnp.zeros((2, NX // 2, NY // 2, NZ // 2), jnp.float32)
    assembled = [slice_ends[0] + prolong(coarse_prev)]
    for slice_number in range(1, N_TM):
        error_est = (restrict(slice_ends[slice_number - 1]) - restrict(start_states[slice_number])) + coarse_prev
        coarse_prev = propagate(error_est)
        assembled.append(slice_ends[slice_number] + prolong(coarse_prev))
    return jnp.stack(assembled)
```

```python
import jax
import jax.numpy as jnp
from jax import lax
from jax.experimental import pallas as pl
from jax.experimental.pallas import tpu as pltpu
from jax.sharding import PartitionSpec as P

MESH = pl.DeviceIdType.MESH
F32 = jnp.float32
BF16 = jnp.bfloat16

ROWS = 12
SIDE = 256
HALF = SIDE // 2
CROWS = ROWS // 2
PAD = 8
CHUNKS = 4
WIDE = SIDE // CHUNKS
SUB = 32
CSUB = 64
SPREAD = 0.08
LAST = 3


def iota(shape, axis):
    return lax.broadcasted_iota(jnp.int32, shape, axis)


def pair_columns(scale):
    match = (iota((SIDE, HALF), 0) // 2) == iota((SIDE, HALF), 1)
    return jnp.where(match, scale, 0.0).astype(BF16)


def pair_rows(scale):
    match = iota((HALF, SIDE), 0) == (iota((HALF, SIDE), 1) // 2)
    return jnp.where(match, scale, 0.0).astype(BF16)


def split(values):
    high = values.astype(BF16)
    return high, (values - high.astype(F32)).astype(BF16)


def dot(left, right):
    return jnp.dot(left, right, preferred_element_type=F32)


def halve(values, rows_table, columns_table):
    high, low = split(values)
    narrow = dot(high, columns_table) + dot(low, columns_table)
    high, low = split(narrow)
    return dot(rows_table, high) + dot(rows_table, low)


def each(count, body):
    lax.fori_loop(0, count, lambda i, _: (body(i), 0)[1], 0)


def main_kernel(
    start, velocity, site_class, attach_table, detach_table,
    ends, g_out,
    ma, mb, p1, n1, p2, n2, p3, n3, cc, al, be, cls,
    snd, hal, st,
    rs_own, rs_next, d_own, dd, g_in,
    mca, mcb, sc, pc1, nc1, pc2, nc2, pc3, nc3, ccc, alc, bec,
    csnd, chal, cst,
    load_sem, snd_sem, hal_sem, st_snd, st_rcv, fw_snd, fw_rcv,
    rs_sem, d_snd, d_rcv, g_sem, c_snd, c_rcv, cst_snd, cst_rcv,
):
    t = lax.axis_index("tm")
    s = lax.axis_index("space")
    has_up = s < 31
    has_dn = s > 0
    up = {"space": jnp.minimum(s + 1, 31)}
    dn = {"space": jnp.maximum(s - 1, 0)}
    core = t % 2
    sibling = {"tm": t + 1 - 2 * core}

    def remote(src, dst, send, recv, to):
        return pltpu.make_async_remote_copy(
            src_ref=src, dst_ref=dst, send_sem=send, recv_sem=recv,
            device_id=to, device_id_type=MESH,
        )

    barrier = pltpu.get_barrier_semaphore()
    for j in (1, 2, 3):
        pl.semaphore_signal(barrier, inc=1, device_id={"tm": (t + j) % 4}, device_id_type=MESH)

    @pl.when(has_up)
    def _():
        pl.semaphore_signal(barrier, inc=1, device_id=up, device_id_type=MESH)

    @pl.when(has_dn)
    def _():
        pl.semaphore_signal(barrier, inc=1, device_id=dn, device_id_type=MESH)

    def loads(i):
        inner = pl.ds(PAD, SIDE)
        pairs = (
            (velocity.at[0, i], p1.at[i + 1]),
            (velocity.at[1, i], p2.at[i]),
            (velocity.at[2, i], p3.at[i]),
            (site_class.at[i], cls.at[i]),
            (start.at[0, i], ma.at[i + 1, inner]),
            (start.at[1, i], ends.at[1, i]),
        )
        return [pltpu.make_async_copy(a, b, load_sem.at[j, i]) for j, (a, b) in enumerate(pairs)]

    def order(k):
        return jnp.where(k % 2 == 0, k // 2, ROWS - 1 - k // 2)

    def start_loads(k):
        for copy in loads(order(k)):
            copy.start()

    each(ROWS, start_loads)

    blank = jnp.zeros((PAD, SIDE), F32)

    def clear(i):
        for ref in (ma, mb):
            ref[i, pl.ds(0, PAD), :] = blank
            ref[i, pl.ds(PAD + SIDE, PAD), :] = blank

    each(ROWS + 2, clear)

    def clear_rows(c):
        rows = pl.ds(PAD + c * SUB, SUB)
        plain = pl.ds(c * SUB, SUB)
        zero = jnp.zeros((SUB, SIDE), F32)
        one = jnp.ones((SUB, SIDE), F32)
        for ref in (ma, mb):
            ref[0, rows, :] = zero
            ref[ROWS + 1, rows, :] = zero
        p1[0, plain, :] = one
        n1[ROWS + 1, plain, :] = one

        @pl.when(jnp.logical_not(has_dn))
        def _():
            st[0, plain, :] = zero
            for k in range(2):
                for lay in range(2):
                    hal[k, 0, lay, plain, :] = zero

        @pl.when(jnp.logical_not(has_up))
        def _():
            st[1, plain, :] = zero
            for k in range(2):
                for lay in range(2):
                    hal[k, 1, lay, plain, :] = zero

    each(SIDE // SUB, clear_rows)

    rows_table = pair_rows(0.25)
    columns_table = pair_columns(0.5)

    def restrict_pair(read):
        return halve(read(0) + read(1), rows_table, columns_table)

    def restrict_shifted(j):
        pc2[j] = restrict_pair(lambda b: p2[2 * j + b])
        pc3[j] = restrict_pair(lambda b: p3[2 * j + b])

    row8 = iota((SUB, SIDE), 0)
    lane = iota((SUB, SIDE), 1)

    def fine_coefs(i):
        def body(c, before):
            y = pl.multiple_of(c * SUB, SUB)
            rows = pl.ds(y, SUB)
            u1 = p1[i + 1, rows, :]
            u2 = p2[i, rows, :]
            u3 = p3[i, rows, :]
            after = p2[i, pl.ds(pl.multiple_of(jnp.minimum(y + SUB, SIDE - PAD), PAD), PAD), :]
            wide = jnp.concatenate([before, u2, after], axis=0)
            wide_plus = jnp.maximum(wide, 0.0) + SPREAD
            wide_minus = wide_plus - wide
            plus1 = jnp.maximum(u1, 0.0) + SPREAD
            minus1 = plus1 - u1
            plus3 = jnp.maximum(u3, 0.0) + SPREAD
            minus3 = plus3 - u3
            kind = cls[i, rows, :]
            attach = jnp.zeros((SUB, SIDE), F32)
            detach = jnp.zeros((SUB, SIDE), F32)
            for level in range(8):
                here = kind == level
                attach = jnp.where(here, attach_table[level], attach)
                detach = jnp.where(here, detach_table[level], detach)
            total = plus1 + minus1 + wide_plus[PAD:PAD + SUB] + wide_minus[PAD:PAD + SUB] + plus3 + minus3
            p1[i + 1, rows, :] = plus1
            n1[i + 1, rows, :] = minus1
            p2[i, rows, :] = jnp.where(row8 + y == 0, 0.0, wide_plus[PAD - 1:PAD - 1 + SUB])
            n2[i, rows, :] = jnp.where(row8 + y == SIDE - 1, 0.0, wide_minus[PAD + 1:PAD + 1 + SUB])
            p3[i, rows, :] = jnp.where(lane == 0, 0.0, pltpu.roll(plus3, 1, 1))
            n3[i, rows, :] = jnp.where(lane == SIDE - 1, 0.0, pltpu.roll(minus3, SIDE - 1, 1))
            cc[i, rows, :] = (1.0 - total) - attach
            al[i, rows, :] = attach
            be[i, rows, :] = detach
            return u2[SUB - PAD:]

        lax.fori_loop(0, SIDE // SUB, body, jnp.zeros((PAD, SIDE), F32))

    sv = ends.at[1]

    def fine_row(src, i, y):
        rows = pl.ds(y, SUB)
        wide = src[i + 1, pl.ds(y, SUB + 2 * PAD), :]
        mid = wide[PAD:PAD + SUB]
        old = sv[i, rows, :]
        off = be[i, rows, :] * old
        padded = pl.ds(y + PAD, SUB)
        out = cc[i, rows, :] * mid + off
        out = out + (p1[i, rows, :] * src[i, padded, :] + n1[i + 2, rows, :] * src[i + 2, padded, :])
        out = out + (p2[i, rows, :] * wide[PAD - 1:PAD - 1 + SUB] + n2[i, rows, :] * wide[PAD + 1:PAD + 1 + SUB])
        out = out + (p3[i, rows, :] * pltpu.roll(mid, 1, 1) + n3[i, rows, :] * pltpu.roll(mid, SIDE - 1, 1))
        return mid, out, (old - off) + al[i, rows, :] * mid

    def step_rows(src, write, first, count, y0, length):
        subs = length // SUB

        def body(n):
            i = first + n // subs
            y = pl.multiple_of(y0 + (n % subs) * SUB, SUB)
            _, out, held = fine_row(src, i, y)
            write(i, y, out)
            sv[i, pl.ds(y, SUB), :] = held

        each(count * subs, body)

    def write_a(i, y, out):
        ma[i + 1, pl.ds(y + PAD, SUB), :] = out

    def write_b(i, y, out):
        mb[i + 1, pl.ds(y + PAD, SUB), :] = out

    def write_end(i, y, out):
        ends[0, i, pl.ds(y, SUB), :] = out

    def attach_edge(i):
        def body(c):
            rows = pl.ds(pl.multiple_of(c * SUB, SUB), SUB)
            mid = ma[i + 1, pl.ds(pl.multiple_of(c * SUB, SUB) + PAD, SUB), :]
            old = sv[i, rows, :]
            sv[i, rows, :] = (old - be[i, rows, :] * old) + al[i, rows, :] * mid

        each(SIDE // SUB, body)

    def edge_copies(k, c):
        rows = pl.ds(c * WIDE, WIDE)
        out = []
        for way, (to, sends, receives) in enumerate(((up, has_up, has_dn), (dn, has_dn, has_up))):
            for lay in range(2):
                out.append((sends, receives, remote(
                    snd.at[way, lay, rows], hal.at[k, way, lay, rows],
                    snd_sem.at[k, way, lay, c], hal_sem.at[k, way, lay, c], to,
                )))
        return out

    def send_edges(k, c):
        for way, i, coef in ((0, ROWS - 1, p1), (1, 0, n1)):
            def body(n, way=way, i=i, coef=coef):
                y = pl.multiple_of(c * WIDE + n * SUB, SUB)
                rows = pl.ds(y, SUB)
                mid, out, _ = fine_row(ma, i, y)
                mb[i + 1, pl.ds(y + PAD, SUB), :] = out
                factor = coef[i + 1, rows, :]
                snd[way, 0, rows, :] = factor * mid
                snd[way, 1, rows, :] = factor * out

            each(WIDE // SUB, body)
        for sends, _, copy in edge_copies(k, c):
            pl.when(sends)(copy.start)

    def take_edges(k, c):
        for _, receives, copy in edge_copies(k, c):
            pl.when(receives)(copy.wait_recv)

        def body(n):
            y = pl.multiple_of(c * WIDE + n * SUB, SUB)
            rows = pl.ds(y, SUB)
            padded = pl.ds(y + PAD, SUB)
            mb[1, padded, :] = mb[1, padded, :] + hal[k, 0, 0, rows, :]
            mb[ROWS, padded, :] = mb[ROWS, padded, :] + hal[k, 1, 0, rows, :]
            mb[0, padded, :] = hal[k, 0, 1, rows, :] + st[0, rows, :] * snd[1, 0, rows, :]
            mb[ROWS + 1, padded, :] = hal[k, 1, 1, rows, :] + st[1, rows, :] * snd[0, 0, rows, :]

        each(WIDE // SUB, body)

    def edge_step(write, c):
        y0 = c * WIDE
        step_rows(mb, write, 0, 2, y0, WIDE)
        step_rows(mb, write, ROWS - 2, 2, y0, WIDE)

    def wait_edges(k, c):
        for sends, _, copy in edge_copies(k, c):
            pl.when(sends)(copy.wait_send)

    def ready(k):
        for copy in loads(order(k)):
            copy.wait()

    each(4, ready)
    restrict_shifted(0)
    restrict_shifted(CROWS - 1)
    each(4, lambda k: fine_coefs(order(k)))

    pl.semaphore_wait(barrier, 3 + has_up.astype(jnp.int32) + has_dn.astype(jnp.int32))

    own_half = pl.ds(core * HALF, HALF)
    other_half = pl.ds((1 - core) * HALF, HALF)
    st_up = remote(p1.at[ROWS, own_half], st.at[0, own_half], st_snd.at[0], st_rcv.at[0], up)
    st_dn = remote(n1.at[1, own_half], st.at[1, own_half], st_snd.at[1], st_rcv.at[1], dn)
    pl.when(has_up)(st_up.start)
    pl.when(has_dn)(st_dn.start)

    each(CHUNKS, lambda c: send_edges(0, c))

    def later(n):
        j = jnp.where(n % 2 == 0, 1 + n // 2, CROWS - 2 - n // 2)
        for b in range(2):
            for copy in loads(2 * j + b):
                copy.wait()
        restrict_shifted(j)
        for b in range(2):
            fine_coefs(2 * j + b)

    each(CROWS - 2, later)

    inner = pl.ds(PAD, SIDE)

    def restrict_start(j):
        rs_own[0, j] = restrict_pair(lambda b: ma[2 * j + b + 1, inner, :])
        rs_own[1, j] = restrict_pair(lambda b: sv[2 * j + b])

    each(CROWS, restrict_start)

    rs_copy = remote(rs_own, rs_next, rs_sem.at[0], rs_sem.at[1], {"tm": (t + 3) % 4})
    pl.when(t > 0)(rs_copy.start)

    def interior(write):
        attach_edge(0)
        attach_edge(ROWS - 1)
        step_rows(ma, write_b, 1, ROWS - 2, 0, SIDE)
        step_rows(mb, write, 2, ROWS - 4, 0, SIDE)

    interior(write_a)

    fw = [remote(st.at[w, own_half], st.at[w, own_half], fw_snd.at[w], fw_rcv.at[w], sibling) for w in range(2)]
    fr = [remote(st.at[w, other_half], st.at[w, other_half], fw_snd.at[w], fw_rcv.at[w], sibling) for w in range(2)]
    for w, exists, copy in ((0, has_dn, st_up), (1, has_up, st_dn)):
        @pl.when(exists)
        def _(w=w, copy=copy):
            copy.wait_recv()
            fw[w].start()
    for w, exists in ((0, has_dn), (1, has_up)):
        pl.when(exists)(fr[w].wait_recv)

    def between(n):
        pl.when(n < CHUNKS)(lambda: take_edges(0, n))
        pl.when(jnp.logical_and(n >= 1, n <= CHUNKS))(lambda: edge_step(write_a, n - 1))

        @pl.when(n >= 2)
        def _():
            wait_edges(0, n - 2)
            send_edges(1, n - 2)

    each(CHUNKS + 2, between)

    interior(write_end)

    def restrict_static(j):
        pc1[j + 1] = restrict_pair(lambda b: p1[2 * j + b + 1] - n1[2 * j + b + 1])
        alc[j] = 2.0 * restrict_pair(lambda b: al[2 * j + b])
        bec[j] = 2.0 * restrict_pair(lambda b: be[2 * j + b])

    crow = iota((HALF, HALF), 0)
    clane = iota((HALF, HALF), 1)
    coarse_spread = 0.5 * SPREAD

    def coarse_coefs(j):
        u1, u2, u3 = pc1[j + 1], pc2[j], pc3[j]
        plus1 = jnp.maximum(u1, 0.0) + coarse_spread
        minus1 = plus1 - u1
        plus2 = jnp.maximum(u2, 0.0) + coarse_spread
        minus2 = plus2 - u2
        plus3 = jnp.maximum(u3, 0.0) + coarse_spread
        minus3 = plus3 - u3
        ccc[j] = (1.0 - (plus1 + minus1 + plus2 + minus2 + plus3 + minus3)) - alc[j]
        pc1[j + 1] = plus1
        nc1[j + 1] = minus1
        pc2[j] = jnp.where(crow == 0, 0.0, pltpu.roll(plus2, 1, 0))
        nc2[j] = jnp.where(crow == HALF - 1, 0.0, pltpu.roll(minus2, HALF - 1, 0))
        pc3[j] = jnp.where(clane == 0, 0.0, pltpu.roll(plus3, 1, 1))
        nc3[j] = jnp.where(clane == HALF - 1, 0.0, pltpu.roll(minus3, HALF - 1, 1))

    is_last = t == LAST
    cst_up = remote(pc1.at[CROWS], cst.at[0], cst_snd.at[0], cst_rcv.at[0], up)
    cst_dn = remote(nc1.at[1], cst.at[1], cst_snd.at[1], cst_rcv.at[1], dn)

    def d_copies(outer):
        out = []
        for comp in range(2):
            if outer:
                places = ((2 + comp, pl.ds(0, 1)), (4 + comp, pl.ds(CROWS - 1, 1)))
            else:
                places = ((comp, pl.ds(1, CROWS - 2)),)
            for n, rows in places:
                out.append(remote(
                    d_own.at[comp, rows], dd.at[t + 1, comp, rows],
                    d_snd.at[n], d_rcv.at[t, n], {"tm": LAST},
                ))
        return out

    def jump(j):
        for comp in range(2):
            d_own[comp, j] = restrict_pair(lambda b: ends[comp, 2 * j + b]) - rs_next[comp, j]

    @pl.when(jnp.logical_not(is_last))
    def _():
        rs_copy.wait_recv()
        each(CROWS - 2, lambda n: jump(n + 1))
        for copy in d_copies(False):
            copy.start()

    @pl.when(is_last)
    def _():
        def body(j):
            restrict_static(j)
            coarse_coefs(j)

        each(CROWS, body)
        pl.when(has_up)(cst_up.start)
        pl.when(has_dn)(cst_dn.start)
        zero = jnp.zeros((HALF, HALF), F32)
        one = jnp.ones((HALF, HALF), F32)
        pc1[0] = one
        nc1[CROWS + 1] = one
        margin = jnp.zeros((PAD, HALF), F32)
        middle = pl.ds(PAD, HALF)

        def margins(j):
            for ref in (mca, mcb):
                ref[j, pl.ds(0, PAD), :] = margin
                ref[j, pl.ds(PAD + HALF, PAD), :] = margin

        each(CROWS + 2, margins)
        for j in (0, CROWS + 1):
            mca[j, middle, :] = zero

        @pl.when(jnp.logical_not(has_dn))
        def _():
            cst[0] = zero
            for k in range(3):
                for lay in range(2):
                    chal[k, 0, lay] = zero

        @pl.when(jnp.logical_not(has_up))
        def _():
            cst[1] = zero
            for k in range(3):
                for lay in range(2):
                    chal[k, 1, lay] = zero

        def clear_first(j):
            dd[0, 0, j] = zero
            dd[0, 1, j] = zero

        each(CROWS, clear_first)

    def finish(n):
        pl.when(n < CHUNKS)(lambda: take_edges(1, n))
        pl.when(n >= 1)(lambda: edge_step(write_end, n - 1))

    each(CHUNKS + 1, finish)

    @pl.when(jnp.logical_not(is_last))
    def _():
        jump(0)
        jump(CROWS - 1)
        for copy in d_copies(True):
            copy.start()

    def coarse_row(src, j, y):
        rows = pl.ds(y, CSUB)
        wide = src[j + 1, pl.ds(y, CSUB + 2 * PAD), :]
        mid = wide[PAD:PAD + CSUB]
        old = sc[j, rows, :]
        off = bec[j, rows, :] * old
        padded = pl.ds(y + PAD, CSUB)
        out = ccc[j, rows, :] * mid + off
        out = out + (pc1[j, rows, :] * src[j, padded, :] + nc1[j + 2, rows, :] * src[j + 2, padded, :])
        out = out + (pc2[j, rows, :] * wide[PAD - 1:PAD - 1 + CSUB] + nc2[j, rows, :] * wide[PAD + 1:PAD + 1 + CSUB])
        out = out + (pc3[j, rows, :] * pltpu.roll(mid, 1, 1) + nc3[j, rows, :] * pltpu.roll(mid, HALF - 1, 1))
        return mid, out, (old - off) + alc[j, rows, :] * mid

    halves = HALF // CSUB

    def coarse_first(j, with_held):
        for c in range(halves):
            y = c * CSUB
            _, out, held = coarse_row(mca, j, y)
            mcb[j + 1, pl.ds(y + PAD, CSUB), :] = out
            if with_held:
                sc[j, pl.ds(y, CSUB), :] = held

    def coarse_second(turn, j):
        for c in range(halves):
            y = c * CSUB
            _, out, held = coarse_row(mcb, j, y)
            dd[turn, 0, j, pl.ds(y, CSUB), :] = out
            dd[turn, 1, j, pl.ds(y, CSUB), :] = held

    def coarse_edge_copies(turn):
        out = []
        for way, (to, sends, receives) in enumerate(((up, has_up, has_dn), (dn, has_dn, has_up))):
            for lay in range(2):
                out.append((sends, receives, remote(
                    csnd.at[turn - 1, way, lay], chal.at[turn - 1, way, lay],
                    c_snd.at[turn - 1, way, lay], c_rcv.at[turn - 1, way, lay], to,
                )))
        return out

    middle = pl.ds(PAD, HALF)

    def chain(turn):
        for comp in range(2):
            for n, rows in ((comp, pl.ds(1, CROWS - 2)), (2 + comp, pl.ds(0, 1)), (4 + comp, pl.ds(CROWS - 1, 1))):
                remote(
                    d_own.at[comp, rows], dd.at[turn, comp, rows],
                    d_snd.at[n], d_rcv.at[turn - 1, n], {"tm": 0},
                ).wait_recv()

        def gather(j):
            mca[j + 1, middle, :] = dd[turn, 0, j] + dd[turn - 1, 0, j]
            sc[j] = dd[turn, 1, j] + dd[turn - 1, 1, j]

        each(CROWS, gather)
        for way, j, coef in ((0, CROWS - 1, pc1), (1, 0, nc1)):
            coarse_first(j, False)
            factor = coef[j + 1]
            csnd[turn - 1, way, 0] = factor * mca[j + 1, middle, :]
            csnd[turn - 1, way, 1] = factor * mcb[j + 1, middle, :]
        for sends, _, copy in coarse_edge_copies(turn):
            pl.when(sends)(copy.start)

        for j in (0, CROWS - 1):
            old = sc[j]
            sc[j] = (old - bec[j] * old) + alc[j] * mca[j + 1, middle, :]
        each(CROWS - 2, lambda n: coarse_first(n + 1, True))
        each(CROWS - 4, lambda n: coarse_second(turn, n + 2))

        @pl.when(turn == 1)
        def _():
            pl.when(has_dn)(cst_up.wait_recv)
            pl.when(has_up)(cst_dn.wait_recv)

        for _, receives, copy in coarse_edge_copies(turn):
            pl.when(receives)(copy.wait_recv)
        mcb[1, middle, :] = mcb[1, middle, :] + chal[turn - 1, 0, 0]
        mcb[CROWS, middle, :] = mcb[CROWS, middle, :] + chal[turn - 1, 1, 0]
        mcb[0, middle, :] = chal[turn - 1, 0, 1] + cst[0] * csnd[turn - 1, 1, 0]
        mcb[CROWS + 1, middle, :] = chal[turn - 1, 1, 1] + cst[1] * csnd[turn - 1, 0, 0]
        each(2, lambda n: coarse_second(turn, n))
        each(2, lambda n: coarse_second(turn, n + CROWS - 2))

        @pl.when(turn < LAST)
        def _():
            remote(dd.at[turn], g_in, g_sem.at[turn - 1], g_sem.at[2], {"tm": turn}).start()

    @pl.when(is_last)
    def _():
        each(3, lambda n: chain(n + 1))

        def result(j):
            g_out[0, j] = dd[LAST, 0, j]
            g_out[1, j] = dd[LAST, 1, j]

        each(CROWS, result)

        def sent(n):
            remote(dd.at[n + 1], g_in, g_sem.at[n], g_sem.at[2], {"tm": n + 1}).wait_send()
            return None

        each(2, sent)

        def edges_sent(n):
            for sends, _, copy in coarse_edge_copies(n + 1):
                pl.when(sends)(copy.wait_send)

        each(3, edges_sent)
        pl.when(has_up)(cst_up.wait_send)
        pl.when(has_dn)(cst_dn.wait_send)

    @pl.when(jnp.logical_not(is_last))
    def _():
        for copy in d_copies(False) + d_copies(True):
            copy.wait_send()

        @pl.when(t > 0)
        def _():
            remote(dd.at[1], g_in, g_sem.at[0], g_sem.at[2], {"tm": LAST}).wait_recv()

            def result(j):
                g_out[0, j] = g_in[0, j]
                g_out[1, j] = g_in[1, j]

            each(CROWS, result)

        @pl.when(t == 0)
        def _():
            def result(j):
                g_out[0, j] = jnp.zeros((HALF, HALF), F32)
                g_out[1, j] = jnp.zeros((HALF, HALF), F32)

            each(CROWS, result)

    each(CHUNKS, lambda c: wait_edges(1, c))
    pl.when(has_up)(st_up.wait_send)
    pl.when(has_dn)(st_dn.wait_send)
    pl.when(has_dn)(fw[0].wait_send)
    pl.when(has_up)(fw[1].wait_send)
    pl.when(t > 0)(rs_copy.wait_send)


def final_kernel(ends, g, out, buf, sem):
    wide = (iota((HALF, SIDE), 0) == (iota((HALF, SIDE), 1) // 2)).astype(F32).astype(BF16)
    tall = ((iota((SIDE, HALF), 0) // 2) == iota((SIDE, HALF), 1)).astype(F32).astype(BF16)

    def copy(comp, i):
        return pltpu.make_async_copy(buf.at[comp, i], out.at[comp, i], sem.at[comp, i])

    def body(n):
        comp, j = n // CROWS, n % CROWS
        spread = None
        for part in split(g[comp, j]):
            term = dot(tall, dot(part, wide).astype(BF16))
            spread = term if spread is None else spread + term
        for b in range(2):
            buf[comp, 2 * j + b] = ends[comp, 2 * j + b] + spread
            copy(comp, 2 * j + b).start()

    each(2 * CROWS, body)
    each(2 * ROWS, lambda n: copy(n // ROWS, n % ROWS).wait())


def per_device(start_states, velocity, site_class, attach_rates, detach_rates):
    any_ref = pl.BlockSpec(memory_space=pl.ANY)
    smem = pl.BlockSpec(memory_space=pltpu.SMEM)
    vmem = pl.BlockSpec(memory_space=pltpu.VMEM)
    start = start_states.reshape(start_states.shape[1:])
    plane = (SIDE, SIDE)
    cplane = (HALF, HALF)
    coarse = (2, CROWS) + cplane

    def buf(*shape):
        return pltpu.VMEM(shape, F32)

    brick = buf(ROWS, *plane)
    cbrick = buf(CROWS, *cplane)
    dma = pltpu.SemaphoreType.DMA
    ends, g = pl.pallas_call(
        main_kernel,
        out_shape=(pltpu.VMEM((2, ROWS) + plane, F32), pltpu.VMEM(coarse, F32)),
        in_specs=[any_ref, any_ref, any_ref, smem, smem],
        out_specs=(vmem, vmem),
        scratch_shapes=[
            buf(ROWS + 2, SIDE + 2 * PAD, SIDE), buf(ROWS + 2, SIDE + 2 * PAD, SIDE),
            buf(ROWS + 2, *plane), buf(ROWS + 2, *plane), brick, brick, brick, brick, brick, brick, brick,
            pltpu.VMEM((ROWS,) + plane, jnp.int32),
            buf(2, 2, *plane), buf(2, 2, 2, *plane), buf(2, *plane),
            buf(*coarse), buf(*coarse), buf(*coarse), buf(4, *coarse), buf(*coarse),
            buf(CROWS + 2, HALF + 2 * PAD, HALF), buf(CROWS + 2, HALF + 2 * PAD, HALF), cbrick,
            buf(CROWS + 2, *cplane), buf(CROWS + 2, *cplane), cbrick, cbrick, cbrick, cbrick, cbrick, cbrick, cbrick,
            buf(3, 2, 2, *cplane), buf(3, 2, 2, *cplane), buf(2, *cplane),
            dma((6, ROWS)), dma((2, 2, 2, CHUNKS)), dma((2, 2, 2, CHUNKS)), dma((2,)), dma((2,)), dma((2,)), dma((2,)),
            dma((2,)), dma((6,)), dma((3, 6)), dma((3,)), dma((3, 2, 2)), dma((3, 2, 2)), dma((2,)), dma((2,)),
        ],
        compiler_params=pltpu.CompilerParams(
            collective_id=0, has_side_effects=True, vmem_limit_bytes=56 * 1024 * 1024
        ),
    )(start, velocity, site_class, attach_rates, detach_rates)
    out = pl.pallas_call(
        final_kernel,
        out_shape=jax.ShapeDtypeStruct((2, ROWS) + plane, F32),
        in_specs=[vmem, vmem],
        out_specs=any_ref,
        scratch_shapes=[buf(2, ROWS, *plane), dma((2, ROWS))],
        compiler_params=pltpu.CompilerParams(vmem_limit_bytes=40 * 1024 * 1024),
    )(ends, g)
    return out[None]


def solution(mesh):
    in_specs = (
        P("tm", None, "space", None, None),
        P(None, "space", None, None),
        P("space", None, None),
        P(),
        P(),
    )
    return jax.shard_map(
        per_device, mesh=mesh, in_specs=in_specs, out_specs=P("tm", None, "space", None, None), check_vma=False
    )
```

```python
import jax
import jax.numpy as jnp
from jax import lax
from jax.experimental import pallas as pl
from jax.experimental.pallas import tpu as pltpu
from jax.sharding import PartitionSpec as P

MESH = pl.DeviceIdType.MESH
F32 = jnp.float32
BF16 = jnp.bfloat16

ROWS = 12
SIDE = 256
HALF = SIDE // 2
CROWS = ROWS // 2
PAD = 8
CHUNKS = 4
WIDE = SIDE // CHUNKS
SUB = 32
COEF = 128
PLANES = 4
SPREAD = 0.08
LAST = 3


def iota(shape, axis):
    return lax.broadcasted_iota(jnp.int32, shape, axis)


def pair_columns(scale):
    match = (iota((SIDE, HALF), 0) // 2) == iota((SIDE, HALF), 1)
    return jnp.where(match, scale, 0.0).astype(BF16)


def split(values):
    high = values.astype(BF16)
    return high, (values - high.astype(F32)).astype(BF16)


def dot(left, right):
    return jnp.dot(left, right, preferred_element_type=F32)


def each(count, body, unroll=1):
    lax.fori_loop(0, count, lambda i, _: (body(i), 0)[1], 0, unroll=unroll)


def main_kernel(
    start, velocity, site_class, attach_table, detach_table,
    ends, g_out,
    ma, mb, p1, n1, p2, n2, p3, n3, cc, al, be, cls,
    snd, hal, st,
    rs_own, rs_next, d_own, dd, g_in,
    mca, mcb, sc, pc1, nc1, pc2, nc2, pc3, nc3, ccc, alc, bec,
    csnd, chal, cst, tmp,
    load_sem, snd_sem, hal_sem, st_snd, st_rcv, fw_snd, fw_rcv,
    rs_sem, d_snd, d_rcv, g_sem, c_snd, c_rcv, cst_snd, cst_rcv,
):
    t = lax.axis_index("tm")
    s = lax.axis_index("space")
    has_up = s < 31
    has_dn = s > 0
    up = {"space": jnp.minimum(s + 1, 31)}
    dn = {"space": jnp.maximum(s - 1, 0)}
    core = t % 2
    sibling = {"tm": t + 1 - 2 * core}

    def remote(src, dst, send, recv, to):
        return pltpu.make_async_remote_copy(
            src_ref=src, dst_ref=dst, send_sem=send, recv_sem=recv,
            device_id=to, device_id_type=MESH,
        )

    barrier = pltpu.get_barrier_semaphore()
    for j in (1, 2, 3):
        pl.semaphore_signal(barrier, inc=1, device_id={"tm": (t + j) % 4}, device_id_type=MESH)

    @pl.when(has_up)
    def _():
        pl.semaphore_signal(barrier, inc=1, device_id=up, device_id_type=MESH)

    @pl.when(has_dn)
    def _():
        pl.semaphore_signal(barrier, inc=1, device_id=dn, device_id_type=MESH)

    def loads(i):
        inner = pl.ds(PAD, SIDE)
        pairs = (
            (velocity.at[0, i], p1.at[i + 1]),
            (velocity.at[1, i], p2.at[i]),
            (velocity.at[2, i], p3.at[i]),
            (site_class.at[i], cls.at[slot(i)]),
            (start.at[0, i], ma.at[i + 1, inner]),
            (start.at[1, i], ends.at[1, i]),
        )
        return [pltpu.make_async_copy(a, b, load_sem.at[j, i]) for j, (a, b) in enumerate(pairs)]

    def slot(i):
        return jnp.where(i < CROWS, 2 * i, 2 * (ROWS - 1 - i) + 1) % 8

    def order(k):
        return jnp.where(k % 2 == 0, k // 2, ROWS - 1 - k // 2)

    def start_loads(k):
        for n, copy in enumerate(loads(order(k))):
            if n != 3:
                copy.start()
            else:
                pl.when(k < 8)(copy.start)

    each(ROWS, start_loads)

    blank = jnp.zeros((PAD, SIDE), F32)

    def clear(i):
        for ref in (ma, mb):
            ref[i, pl.ds(0, PAD), :] = blank
            ref[i, pl.ds(PAD + SIDE, PAD), :] = blank

    each(ROWS + 2, clear)

    def clear_rows(c):
        rows = pl.ds(PAD + c * SUB, SUB)
        plain = pl.ds(c * SUB, SUB)
        zero = jnp.zeros((SUB, SIDE), F32)
        one = jnp.ones((SUB, SIDE), F32)
        for ref in (ma, mb):
            ref[0, rows, :] = zero
            ref[ROWS + 1, rows, :] = zero
        p1[0, plain, :] = one
        n1[ROWS + 1, plain, :] = one

        @pl.when(jnp.logical_not(has_dn))
        def _():
            st[0, plain, :] = zero
            for k in range(2):
                for lay in range(2):
                    hal[k, 0, lay, plain, :] = zero

        @pl.when(jnp.logical_not(has_up))
        def _():
            st[1, plain, :] = zero
            for k in range(2):
                for lay in range(2):
                    hal[k, 1, lay, plain, :] = zero

    each(SIDE // SUB, clear_rows)

    columns_table = pair_columns(0.125)

    def restrict_pairs(items):
        for n, (read, _) in enumerate(items):
            high, low = split(read(0) + read(1))
            tmp[n] = dot(high, columns_table) + dot(low, columns_table)
        for n, (_, write) in enumerate(items):
            write(tmp[n, pl.ds(0, HALF, 2), :] + tmp[n, pl.ds(1, HALF, 2), :])

    def put(ref, *index):
        def write(value):
            ref[index] = value
        return write

    def restrict_shifted(*pairs):
        items = []
        for j in pairs:
            items.append((lambda b, j=j: p2[2 * j + b], put(pc2, j)))
            items.append((lambda b, j=j: p3[2 * j + b], put(pc3, j)))
        restrict_pairs(items)

    row8 = iota((COEF, SIDE), 0)
    lane = iota((COEF, SIDE), 1)

    def fine_coefs(i):
        def body(c, before):
            y = pl.multiple_of(c * COEF, COEF)
            rows = pl.ds(y, COEF)
            u1 = p1[i + 1, rows, :]
            u2 = p2[i, rows, :]
            u3 = p3[i, rows, :]
            after = p2[i, pl.ds(pl.multiple_of(jnp.minimum(y + COEF, SIDE - PAD), PAD), PAD), :]
            wide = jnp.concatenate([before, u2, after], axis=0)
            wide_plus = jnp.maximum(wide, 0.0) + SPREAD
            wide_minus = wide_plus - wide
            plus1 = jnp.maximum(u1, 0.0) + SPREAD
            minus1 = plus1 - u1
            plus3 = jnp.maximum(u3, 0.0) + SPREAD
            minus3 = plus3 - u3
            kind = cls[slot(i), rows, :]
            attach = jnp.zeros((COEF, SIDE), F32)
            detach = jnp.zeros((COEF, SIDE), F32)
            for level in range(8):
                here = kind == level
                attach = jnp.where(here, attach_table[level], attach)
                detach = jnp.where(here, detach_table[level], detach)
            total = plus1 + minus1 + wide_plus[PAD:PAD + COEF] + wide_minus[PAD:PAD + COEF] + plus3 + minus3
            p1[i + 1, rows, :] = plus1
            n1[i + 1, rows, :] = minus1
            p2[i, rows, :] = jnp.where(row8 + y == 0, 0.0, wide_plus[PAD - 1:PAD - 1 + COEF])
            n2[i, rows, :] = jnp.where(row8 + y == SIDE - 1, 0.0, wide_minus[PAD + 1:PAD + 1 + COEF])
            p3[i, rows, :] = jnp.where(lane == 0, 0.0, pltpu.roll(plus3, 1, 1))
            n3[i, rows, :] = jnp.where(lane == SIDE - 1, 0.0, pltpu.roll(minus3, SIDE - 1, 1))
            cc[i, rows, :] = (1.0 - total) - attach
            al[i, rows, :] = attach
            be[i, rows, :] = detach
            return u2[COEF - PAD:]

        lax.fori_loop(0, SIDE // COEF, body, jnp.zeros((PAD, SIDE), F32), unroll=SIDE // COEF)

    sv = ends.at[1]

    def fine_row(src, i, y, size):
        rows = pl.ds(y, size)
        wide = src[i + 1, pl.ds(y, size + 2 * PAD), :]
        mid = wide[PAD:PAD + size]
        old = sv[i, rows, :]
        off = be[i, rows, :] * old
        padded = pl.ds(y + PAD, size)
        out = cc[i, rows, :] * mid + off
        out = out + (p1[i, rows, :] * src[i, padded, :] + n1[i + 2, rows, :] * src[i + 2, padded, :])
        out = out + (p2[i, rows, :] * wide[PAD - 1:PAD - 1 + size] + n2[i, rows, :] * wide[PAD + 1:PAD + 1 + size])
        out = out + (p3[i, rows, :] * pltpu.roll(mid, 1, 1) + n3[i, rows, :] * pltpu.roll(mid, SIDE - 1, 1))
        return mid, out, (old - off) + al[i, rows, :] * mid

    def step_row(src, write, i, y, size):
        _, out, held = fine_row(src, i, y, size)
        write(i, y, size, out)
        sv[i, pl.ds(y, size), :] = held

    def write_a(i, y, size, out):
        ma[i + 1, pl.ds(y + PAD, size), :] = out

    def write_b(i, y, size, out):
        mb[i + 1, pl.ds(y + PAD, size), :] = out

    def write_end(i, y, size, out):
        ends[0, i, pl.ds(y, size), :] = out

    def attach_edge(i):
        old = sv[i]
        sv[i] = (old - be[i] * old) + al[i] * ma[i + 1, pl.ds(PAD, SIDE), :]

    def edge_copies(k, c):
        rows = pl.ds(c * WIDE, WIDE)
        out = []
        for way, (to, sends, receives) in enumerate(((up, has_up, has_dn), (dn, has_dn, has_up))):
            for lay in range(2):
                out.append((sends, receives, remote(
                    snd.at[way, lay, rows], hal.at[k, way, lay, rows],
                    snd_sem.at[k, way, lay, c], hal_sem.at[k, way, lay, c], to,
                )))
        return out

    def send_edges(k, c):
        y = pl.multiple_of(c * WIDE, WIDE)
        rows = pl.ds(y, WIDE)
        for way, i, coef in ((0, ROWS - 1, p1), (1, 0, n1)):
            mid, out, _ = fine_row(ma, i, y, WIDE)
            mb[i + 1, pl.ds(y + PAD, WIDE), :] = out
            factor = coef[i + 1, rows, :]
            snd[way, 0, rows, :] = factor * mid
            snd[way, 1, rows, :] = factor * out
        for sends, _, copy in edge_copies(k, c):
            pl.when(sends)(copy.start)

    def take_edges(k, c):
        for _, receives, copy in edge_copies(k, c):
            pl.when(receives)(copy.wait_recv)

        y = pl.multiple_of(c * WIDE, WIDE)
        rows = pl.ds(y, WIDE)
        padded = pl.ds(y + PAD, WIDE)
        mb[1, padded, :] = mb[1, padded, :] + hal[k, 0, 0, rows, :]
        mb[ROWS, padded, :] = mb[ROWS, padded, :] + hal[k, 1, 0, rows, :]
        mb[0, padded, :] = hal[k, 0, 1, rows, :] + st[0, rows, :] * snd[1, 0, rows, :]
        mb[ROWS + 1, padded, :] = hal[k, 1, 1, rows, :] + st[1, rows, :] * snd[0, 0, rows, :]

    def edge_step(write, c):
        y = pl.multiple_of(c * WIDE, WIDE)
        for i in (0, ROWS - 1, 1, ROWS - 2):
            step_row(mb, write, i, y, WIDE)

    def wait_edges(k, c):
        for sends, _, copy in edge_copies(k, c):
            pl.when(sends)(copy.wait_send)

    def ready(k):
        for copy in loads(order(k)):
            copy.wait()

    each(4, ready)
    restrict_shifted(0, CROWS - 1)
    each(4, lambda k: fine_coefs(order(k)))
    each(4, lambda k: loads(order(k + 8))[3].start())

    pl.semaphore_wait(barrier, 3 + has_up.astype(jnp.int32) + has_dn.astype(jnp.int32))

    own_half = pl.ds(core * HALF, HALF)
    other_half = pl.ds((1 - core) * HALF, HALF)
    st_up = remote(p1.at[ROWS, own_half], st.at[0, own_half], st_snd.at[0], st_rcv.at[0], up)
    st_dn = remote(n1.at[1, own_half], st.at[1, own_half], st_snd.at[1], st_rcv.at[1], dn)
    pl.when(has_up)(st_up.start)
    pl.when(has_dn)(st_dn.start)

    each(CHUNKS, lambda c: send_edges(0, c))

    def later(n):
        pairs = (n + 1, CROWS - 2 - n)
        for j in pairs:
            for b in range(2):
                for copy in loads(2 * j + b):
                    copy.wait()
        restrict_shifted(*pairs)
        for j in pairs:
            for b in range(2):
                fine_coefs(2 * j + b)

    each(2, later)

    inner = pl.ds(PAD, SIDE)

    def restrict_start(n):
        items = []
        for j in (2 * n, 2 * n + 1):
            items.append((lambda b, j=j: ma[2 * j + b + 1, inner, :], put(rs_own, 0, j)))
            items.append((lambda b, j=j: sv[2 * j + b], put(rs_own, 1, j)))
        restrict_pairs(items)

    each(CROWS // 2, restrict_start)

    rs_copy = remote(rs_own, rs_next, rs_sem.at[0], rs_sem.at[1], {"tm": (t + 3) % 4})
    pl.when(t > 0)(rs_copy.start)

    def interior(write):
        attach_edge(0)
        attach_edge(ROWS - 1)
        each(ROWS - 2, lambda n: step_row(ma, write_b, n + 1, 0, SIDE), unroll=2)
        each(ROWS - 4, lambda n: step_row(mb, write, n + 2, 0, SIDE), unroll=2)

    interior(write_a)

    fw = [remote(st.at[w, own_half], st.at[w, own_half], fw_snd.at[w], fw_rcv.at[w], sibling) for w in range(2)]
    fr = [remote(st.at[w, other_half], st.at[w, other_half], fw_snd.at[w], fw_rcv.at[w], sibling) for w in range(2)]
    for w, exists, copy in ((0, has_dn, st_up), (1, has_up, st_dn)):
        @pl.when(exists)
        def _(w=w, copy=copy):
            copy.wait_recv()
            fw[w].start()
    for w, exists in ((0, has_dn), (1, has_up)):
        pl.when(exists)(fr[w].wait_recv)

    def between(n):
        pl.when(n < CHUNKS)(lambda: take_edges(0, n))
        pl.when(jnp.logical_and(n >= 1, n <= CHUNKS))(lambda: edge_step(write_a, n - 1))

        @pl.when(n >= 2)
        def _():
            wait_edges(0, n - 2)
            send_edges(1, n - 2)

    each(CHUNKS + 2, between)

    interior(write_end)

    def restrict_static(j):
        restrict_pairs((
            (lambda b: p1[2 * j + b + 1] - n1[2 * j + b + 1], put(pc1, j + 1)),
            (lambda b: 2.0 * al[2 * j + b], put(alc, j)),
            (lambda b: 2.0 * be[2 * j + b], put(bec, j)),
        ))

    crow = iota((HALF, HALF), 0)
    clane = iota((HALF, HALF), 1)
    coarse_spread = 0.5 * SPREAD

    def coarse_coefs(j):
        u1, u2, u3 = pc1[j + 1], pc2[j], pc3[j]
        plus1 = jnp.maximum(u1, 0.0) + coarse_spread
        minus1 = plus1 - u1
        plus2 = jnp.maximum(u2, 0.0) + coarse_spread
        minus2 = plus2 - u2
        plus3 = jnp.maximum(u3, 0.0) + coarse_spread
        minus3 = plus3 - u3
        ccc[j] = (1.0 - (plus1 + minus1 + plus2 + minus2 + plus3 + minus3)) - alc[j]
        pc1[j + 1] = plus1
        nc1[j + 1] = minus1
        pc2[j] = jnp.where(crow == 0, 0.0, pltpu.roll(plus2, 1, 0))
        nc2[j] = jnp.where(crow == HALF - 1, 0.0, pltpu.roll(minus2, HALF - 1, 0))
        pc3[j] = jnp.where(clane == 0, 0.0, pltpu.roll(plus3, 1, 1))
        nc3[j] = jnp.where(clane == HALF - 1, 0.0, pltpu.roll(minus3, HALF - 1, 1))

    is_last = t == LAST
    cst_up = remote(pc1.at[CROWS], cst.at[0], cst_snd.at[0], cst_rcv.at[0], up)
    cst_dn = remote(nc1.at[1], cst.at[1], cst_snd.at[1], cst_rcv.at[1], dn)

    def d_copies(outer):
        out = []
        for comp in range(2):
            if outer:
                places = ((2 + comp, pl.ds(0, 1)), (4 + comp, pl.ds(CROWS - 1, 1)))
            else:
                places = ((comp, pl.ds(1, CROWS - 2)),)
            for n, rows in places:
                out.append(remote(
                    d_own.at[comp, rows], dd.at[t + 1, comp, rows],
                    d_snd.at[n], d_rcv.at[t, n], {"tm": LAST},
                ))
        return out

    def jump(*rows):
        def item(comp, j):
            def write(value):
                d_own[comp, j] = value - rs_next[comp, j]
            return lambda b: ends[comp, 2 * j + b], write

        restrict_pairs([item(comp, j) for j in rows for comp in range(2)])

    @pl.when(jnp.logical_not(is_last))
    def _():
        rs_copy.wait_recv()
        each(2, lambda n: jump(2 * n + 1, 2 * n + 2))
        for copy in d_copies(False):
            copy.start()

    @pl.when(is_last)
    def _():
        def body(j):
            restrict_static(j)
            coarse_coefs(j)

        each(CROWS, body)
        pl.when(has_up)(cst_up.start)
        pl.when(has_dn)(cst_dn.start)
        zero = jnp.zeros((HALF, HALF), F32)
        one = jnp.ones((HALF, HALF), F32)
        pc1[0] = one
        nc1[CROWS + 1] = one
        margin = jnp.zeros((PAD, HALF), F32)
        middle = pl.ds(PAD, HALF)

        def margins(j):
            for ref in (mca, mcb):
                ref[j, pl.ds(0, PAD), :] = margin
                ref[j, pl.ds(PAD + HALF, PAD), :] = margin

        each(CROWS + 2, margins)
        for j in (0, CROWS + 1):
            mca[j, middle, :] = zero

        @pl.when(jnp.logical_not(has_dn))
        def _():
            cst[0] = zero
            for k in range(3):
                for lay in range(2):
                    chal[k, 0, lay] = zero

        @pl.when(jnp.logical_not(has_up))
        def _():
            cst[1] = zero
            for k in range(3):
                for lay in range(2):
                    chal[k, 1, lay] = zero

        def clear_first(j):
            dd[0, 0, j] = zero
            dd[0, 1, j] = zero

        each(CROWS, clear_first)

    def finish(n):
        pl.when(n < CHUNKS)(lambda: take_edges(1, n))
        pl.when(n >= 1)(lambda: edge_step(write_end, n - 1))

    each(CHUNKS + 1, finish)

    @pl.when(jnp.logical_not(is_last))
    def _():
        jump(0, CROWS - 1)
        for copy in d_copies(True):
            copy.start()

    middle = pl.ds(PAD, HALF)

    def coarse_row(src, j):
        wide = src[j + 1]
        mid = wide[PAD:PAD + HALF]
        old = sc[j]
        off = bec[j] * old
        out = ccc[j] * mid + off
        out = out + (pc1[j] * src[j, middle, :] + nc1[j + 2] * src[j + 2, middle, :])
        out = out + (pc2[j] * wide[PAD - 1:PAD - 1 + HALF] + nc2[j] * wide[PAD + 1:PAD + 1 + HALF])
        out = out + (pc3[j] * pltpu.roll(mid, 1, 1) + nc3[j] * pltpu.roll(mid, HALF - 1, 1))
        return mid, out, (old - off) + alc[j] * mid

    def coarse_second(turn, *rows):
        for j in rows:
            _, out, held = coarse_row(mcb, j)
            dd[turn, 0, j] = out
            dd[turn, 1, j] = held

    def coarse_edge_copies(turn):
        out = []
        for way, (to, sends, receives) in enumerate(((up, has_up, has_dn), (dn, has_dn, has_up))):
            for lay in range(2):
                out.append((sends, receives, remote(
                    csnd.at[way, lay], chal.at[turn - 1, way, lay],
                    c_snd.at[turn - 1, way, lay], c_rcv.at[turn - 1, way, lay], to,
                )))
        return out

    def chain(turn):
        for comp in range(2):
            for n, rows in ((comp, pl.ds(1, CROWS - 2)), (2 + comp, pl.ds(0, 1)), (4 + comp, pl.ds(CROWS - 1, 1))):
                remote(
                    d_own.at[comp, rows], dd.at[turn, comp, rows],
                    d_snd.at[n], d_rcv.at[turn - 1, n], {"tm": 0},
                ).wait_recv()

        def gather(j):
            mca[j + 1, middle, :] = dd[turn, 0, j] + dd[turn - 1, 0, j]
            sc[j] = dd[turn, 1, j] + dd[turn - 1, 1, j]

        each(CROWS, gather)
        @pl.when(turn > 1)
        def _():
            for sends, _, copy in coarse_edge_copies(turn - 1):
                pl.when(sends)(copy.wait_send)

        for way, j, coef in ((0, CROWS - 1, pc1), (1, 0, nc1)):
            mid, out, _ = coarse_row(mca, j)
            mcb[j + 1, middle, :] = out
            factor = coef[j + 1]
            csnd[way, 0] = factor * mid
            csnd[way, 1] = factor * out
        for sends, _, copy in coarse_edge_copies(turn):
            pl.when(sends)(copy.start)

        for j in (0, CROWS - 1):
            old = sc[j]
            sc[j] = (old - bec[j] * old) + alc[j] * mca[j + 1, middle, :]
        for j in range(1, CROWS - 1):
            _, out, held = coarse_row(mca, j)
            mcb[j + 1, middle, :] = out
            sc[j] = held
        coarse_second(turn, *range(2, CROWS - 2))

        @pl.when(turn == 1)
        def _():
            pl.when(has_dn)(cst_up.wait_recv)
            pl.when(has_up)(cst_dn.wait_recv)

        for _, receives, copy in coarse_edge_copies(turn):
            pl.when(receives)(copy.wait_recv)
        mcb[1, middle, :] = mcb[1, middle, :] + chal[turn - 1, 0, 0]
        mcb[CROWS, middle, :] = mcb[CROWS, middle, :] + chal[turn - 1, 1, 0]
        mcb[0, middle, :] = chal[turn - 1, 0, 1] + cst[0] * csnd[1, 0]
        mcb[CROWS + 1, middle, :] = chal[turn - 1, 1, 1] + cst[1] * csnd[0, 0]
        coarse_second(turn, 0, CROWS - 1, 1, CROWS - 2)

        @pl.when(turn < LAST)
        def _():
            remote(dd.at[turn], g_in, g_sem.at[turn - 1], g_sem.at[2], {"tm": turn}).start()

    @pl.when(is_last)
    def _():
        each(3, lambda n: chain(n + 1))

        def result(j):
            g_out[0, j] = dd[LAST, 0, j]
            g_out[1, j] = dd[LAST, 1, j]

        each(CROWS, result)

        def sent(n):
            remote(dd.at[n + 1], g_in, g_sem.at[n], g_sem.at[2], {"tm": n + 1}).wait_send()
            return None

        each(2, sent)

        for sends, _, copy in coarse_edge_copies(LAST):
            pl.when(sends)(copy.wait_send)

        pl.when(has_up)(cst_up.wait_send)
        pl.when(has_dn)(cst_dn.wait_send)

    @pl.when(jnp.logical_not(is_last))
    def _():
        for copy in d_copies(False) + d_copies(True):
            copy.wait_send()

        @pl.when(t > 0)
        def _():
            remote(dd.at[1], g_in, g_sem.at[0], g_sem.at[2], {"tm": LAST}).wait_recv()

            def result(j):
                g_out[0, j] = g_in[0, j]
                g_out[1, j] = g_in[1, j]

            each(CROWS, result)

        @pl.when(t == 0)
        def _():
            def result(j):
                g_out[0, j] = jnp.zeros((HALF, HALF), F32)
                g_out[1, j] = jnp.zeros((HALF, HALF), F32)

            each(CROWS, result)

    each(CHUNKS, lambda c: wait_edges(1, c))
    pl.when(has_up)(st_up.wait_send)
    pl.when(has_dn)(st_dn.wait_send)
    pl.when(has_dn)(fw[0].wait_send)
    pl.when(has_up)(fw[1].wait_send)
    pl.when(t > 0)(rs_copy.wait_send)


def final_kernel(ends, g, out, buf, sem):
    wide = (iota((HALF, SIDE), 0) == (iota((HALF, SIDE), 1) // 2)).astype(F32).astype(BF16)
    tall = ((iota((SIDE, HALF), 0) // 2) == iota((SIDE, HALF), 1)).astype(F32).astype(BF16)

    def copy(comp, i):
        return pltpu.make_async_copy(buf.at[comp, i], out.at[comp, i], sem.at[comp, i])

    def body(n):
        comp, j = n // CROWS, n % CROWS
        spread = None
        for part in split(g[comp, j]):
            term = dot(tall, dot(part, wide).astype(BF16))
            spread = term if spread is None else spread + term
        for b in range(2):
            buf[comp, 2 * j + b] = ends[comp, 2 * j + b] + spread
            copy(comp, 2 * j + b).start()

    each(2 * CROWS, body, unroll=2)
    each(2 * ROWS, lambda n: copy(n // ROWS, n % ROWS).wait())


def per_device(start_states, velocity, site_class, attach_rates, detach_rates):
    any_ref = pl.BlockSpec(memory_space=pl.ANY)
    smem = pl.BlockSpec(memory_space=pltpu.SMEM)
    vmem = pl.BlockSpec(memory_space=pltpu.VMEM)
    start = start_states.reshape(start_states.shape[1:])
    plane = (SIDE, SIDE)
    cplane = (HALF, HALF)
    coarse = (2, CROWS) + cplane

    def buf(*shape):
        return pltpu.VMEM(shape, F32)

    brick = buf(ROWS, *plane)
    cbrick = buf(CROWS, *cplane)
    dma = pltpu.SemaphoreType.DMA
    ends, g = pl.pallas_call(
        main_kernel,
        out_shape=(pltpu.VMEM((2, ROWS) + plane, F32), pltpu.VMEM(coarse, F32)),
        in_specs=[any_ref, any_ref, any_ref, smem, smem],
        out_specs=(vmem, vmem),
        scratch_shapes=[
            buf(ROWS + 2, SIDE + 2 * PAD, SIDE), buf(ROWS + 2, SIDE + 2 * PAD, SIDE),
            buf(ROWS + 2, *plane), buf(ROWS + 2, *plane), brick, brick, brick, brick, brick, brick, brick,
            pltpu.VMEM((8,) + plane, jnp.int32),
            buf(2, 2, *plane), buf(2, 2, 2, *plane), buf(2, *plane),
            buf(*coarse), buf(*coarse), buf(*coarse), buf(4, *coarse), buf(*coarse),
            buf(CROWS + 2, HALF + 2 * PAD, HALF), buf(CROWS + 2, HALF + 2 * PAD, HALF), cbrick,
            buf(CROWS + 2, *cplane), buf(CROWS + 2, *cplane), cbrick, cbrick, cbrick, cbrick, cbrick, cbrick, cbrick,
            buf(2, 2, *cplane), buf(3, 2, 2, *cplane), buf(2, *cplane), buf(PLANES, SIDE, HALF),
            dma((6, ROWS)), dma((2, 2, 2, CHUNKS)), dma((2, 2, 2, CHUNKS)), dma((2,)), dma((2,)), dma((2,)), dma((2,)),
            dma((2,)), dma((6,)), dma((3, 6)), dma((3,)), dma((3, 2, 2)), dma((3, 2, 2)), dma((2,)), dma((2,)),
        ],
        compiler_params=pltpu.CompilerParams(
            collective_id=0, has_side_effects=True, vmem_limit_bytes=56 * 1024 * 1024
        ),
    )(start, velocity, site_class, attach_rates, detach_rates)
    out = pl.pallas_call(
        final_kernel,
        out_shape=jax.ShapeDtypeStruct((2, ROWS) + plane, F32),
        in_specs=[vmem, vmem],
        out_specs=any_ref,
        scratch_shapes=[buf(2, ROWS, *plane), dma((2, ROWS))],
        compiler_params=pltpu.CompilerParams(vmem_limit_bytes=40 * 1024 * 1024),
    )(ends, g)
    return out[None]


def solution(mesh):
    in_specs = (
        P("tm", None, "space", None, None),
        P(None, "space", None, None),
        P("space", None, None),
        P(),
        P(),
    )
    return jax.shard_map(
        per_device, mesh=mesh, in_specs=in_specs, out_specs=P("tm", None, "space", None, None), check_vma=False
    )
```

```python
import jax
import jax.numpy as jnp
from jax import lax
from jax.experimental import pallas as pl
from jax.experimental.pallas import tpu as pltpu
from jax.sharding import PartitionSpec as P

MESH = pl.DeviceIdType.MESH
F32 = jnp.float32
BF16 = jnp.bfloat16

ROWS = 12
SIDE = 256
HALF = SIDE // 2
CROWS = ROWS // 2
PAD = 8
CHUNKS = 8
WIDE = SIDE // CHUNKS
SUB = 32
COEF = 128
PLANES = 4
SPREAD = 0.08
LAST = 3


def iota(shape, axis):
    return lax.broadcasted_iota(jnp.int32, shape, axis)


def pair_columns(scale):
    match = (iota((SIDE, HALF), 0) // 2) == iota((SIDE, HALF), 1)
    return jnp.where(match, scale, 0.0).astype(BF16)


def split(values):
    high = values.astype(BF16)
    return high, (values - high.astype(F32)).astype(BF16)


def dot(left, right):
    return jnp.dot(left, right, preferred_element_type=F32)


def each(count, body, unroll=1):
    lax.fori_loop(0, count, lambda i, _: (body(i), 0)[1], 0, unroll=unroll)


def main_kernel(
    start, velocity, site_class, attach_table, detach_table,
    ends, g_out,
    ma, mb, p1, n1, p2, n2, p3, n3, cc, al, be, cls,
    snd, hal, st,
    rs_own, rs_next, d_own, dd, g_in,
    mca, mcb, sc, pc1, nc1, pc2, nc2, pc3, nc3, ccc, alc, bec,
    csnd, chal, cst, tmp,
    load_sem, snd_sem, hal_sem, st_snd, st_rcv, fw_snd, fw_rcv,
    rs_sem, turn_sem, d_snd, d_rcv, g_sem, c_snd, c_rcv, cst_snd, cst_rcv,
):
    t = lax.axis_index("tm")
    s = lax.axis_index("space")
    has_up = s < 31
    has_dn = s > 0
    up = {"space": jnp.minimum(s + 1, 31)}
    dn = {"space": jnp.maximum(s - 1, 0)}
    core = t % 2
    sibling = {"tm": t + 1 - 2 * core}

    def remote(src, dst, send, recv, to):
        return pltpu.make_async_remote_copy(
            src_ref=src, dst_ref=dst, send_sem=send, recv_sem=recv,
            device_id=to, device_id_type=MESH,
        )

    barrier = pltpu.get_barrier_semaphore()
    for j in (1, 2, 3):
        pl.semaphore_signal(barrier, inc=1, device_id={"tm": (t + j) % 4}, device_id_type=MESH)

    @pl.when(has_up)
    def _():
        pl.semaphore_signal(barrier, inc=1, device_id=up, device_id_type=MESH)

    @pl.when(has_dn)
    def _():
        pl.semaphore_signal(barrier, inc=1, device_id=dn, device_id_type=MESH)

    def loads(i):
        inner = pl.ds(PAD, SIDE)
        pairs = (
            (velocity.at[0, i], p1.at[i + 1]),
            (velocity.at[1, i], p2.at[i]),
            (velocity.at[2, i], p3.at[i]),
            (site_class.at[i], cls.at[slot(i)]),
            (start.at[0, i], ma.at[i + 1, inner]),
            (start.at[1, i], ends.at[1, i]),
        )
        return [pltpu.make_async_copy(a, b, load_sem.at[j, i]) for j, (a, b) in enumerate(pairs)]

    def slot(i):
        return jnp.where(i < CROWS, 2 * i, 2 * (ROWS - 1 - i) + 1) % 8

    def order(k):
        return jnp.where(k % 2 == 0, k // 2, ROWS - 1 - k // 2)

    def start_loads(k):
        for copy in loads(order(k)):
            copy.start()

    each(4, start_loads)

    blank = jnp.zeros((PAD, SIDE), F32)

    def clear(i):
        for ref in (ma, mb):
            ref[i, pl.ds(0, PAD), :] = blank
            ref[i, pl.ds(PAD + SIDE, PAD), :] = blank

    each(ROWS + 2, clear)

    def clear_rows(c):
        rows = pl.ds(PAD + c * SUB, SUB)
        plain = pl.ds(c * SUB, SUB)
        zero = jnp.zeros((SUB, SIDE), F32)
        one = jnp.ones((SUB, SIDE), F32)
        for ref in (ma, mb):
            ref[0, rows, :] = zero
            ref[ROWS + 1, rows, :] = zero
        p1[0, plain, :] = one
        n1[ROWS + 1, plain, :] = one

        @pl.when(jnp.logical_not(has_dn))
        def _():
            st[0, plain, :] = zero
            for k in range(2):
                for lay in range(2):
                    hal[k, 0, lay, plain, :] = zero

        @pl.when(jnp.logical_not(has_up))
        def _():
            st[1, plain, :] = zero
            for k in range(2):
                for lay in range(2):
                    hal[k, 1, lay, plain, :] = zero

    each(SIDE // SUB, clear_rows)

    columns_table = pair_columns(0.125)

    def restrict_pairs(items):
        for n, (read, _) in enumerate(items):
            high, low = split(read(0) + read(1))
            tmp[n] = dot(high, columns_table) + dot(low, columns_table)
        for n, (_, write) in enumerate(items):
            write(tmp[n, pl.ds(0, HALF, 2), :] + tmp[n, pl.ds(1, HALF, 2), :])

    def put(ref, *index):
        def write(value):
            ref[index] = value
        return write

    def restrict_shifted(*pairs):
        items = []
        for j in pairs:
            items.append((lambda b, j=j: p2[2 * j + b], put(pc2, j)))
            items.append((lambda b, j=j: p3[2 * j + b], put(pc3, j)))
        restrict_pairs(items)

    row8 = iota((COEF, SIDE), 0)
    lane = iota((COEF, SIDE), 1)

    def fine_coefs(i):
        def body(c, before):
            y = pl.multiple_of(c * COEF, COEF)
            rows = pl.ds(y, COEF)
            u1 = p1[i + 1, rows, :]
            u2 = p2[i, rows, :]
            u3 = p3[i, rows, :]
            after = p2[i, pl.ds(pl.multiple_of(jnp.minimum(y + COEF, SIDE - PAD), PAD), PAD), :]
            wide = jnp.concatenate([before, u2, after], axis=0)
            wide_plus = jnp.maximum(wide, 0.0) + SPREAD
            wide_minus = wide_plus - wide
            plus1 = jnp.maximum(u1, 0.0) + SPREAD
            minus1 = plus1 - u1
            plus3 = jnp.maximum(u3, 0.0) + SPREAD
            minus3 = plus3 - u3
            kind = cls[slot(i), rows, :]
            attach = jnp.zeros((COEF, SIDE), F32)
            detach = jnp.zeros((COEF, SIDE), F32)
            for level in range(8):
                here = kind == level
                attach = jnp.where(here, attach_table[level], attach)
                detach = jnp.where(here, detach_table[level], detach)
            total = plus1 + minus1 + wide_plus[PAD:PAD + COEF] + wide_minus[PAD:PAD + COEF] + plus3 + minus3
            p1[i + 1, rows, :] = plus1
            n1[i + 1, rows, :] = minus1
            p2[i, rows, :] = jnp.where(row8 + y == 0, 0.0, wide_plus[PAD - 1:PAD - 1 + COEF])
            n2[i, rows, :] = jnp.where(row8 + y == SIDE - 1, 0.0, wide_minus[PAD + 1:PAD + 1 + COEF])
            p3[i, rows, :] = jnp.where(lane == 0, 0.0, pltpu.roll(plus3, 1, 1))
            n3[i, rows, :] = jnp.where(lane == SIDE - 1, 0.0, pltpu.roll(minus3, SIDE - 1, 1))
            cc[i, rows, :] = (1.0 - total) - attach
            al[i, rows, :] = attach
            be[i, rows, :] = detach
            return u2[COEF - PAD:]

        lax.fori_loop(0, SIDE // COEF, body, jnp.zeros((PAD, SIDE), F32), unroll=SIDE // COEF)

    sv = ends.at[1]

    def fine_row(src, i, y, size):
        rows = pl.ds(y, size)
        wide = src[i + 1, pl.ds(y, size + 2 * PAD), :]
        mid = wide[PAD:PAD + size]
        old = sv[i, rows, :]
        off = be[i, rows, :] * old
        padded = pl.ds(y + PAD, size)
        out = cc[i, rows, :] * mid + off
        out = out + (p1[i, rows, :] * src[i, padded, :] + n1[i + 2, rows, :] * src[i + 2, padded, :])
        out = out + (p2[i, rows, :] * wide[PAD - 1:PAD - 1 + size] + n2[i, rows, :] * wide[PAD + 1:PAD + 1 + size])
        out = out + (p3[i, rows, :] * pltpu.roll(mid, 1, 1) + n3[i, rows, :] * pltpu.roll(mid, SIDE - 1, 1))
        return mid, out, (old - off) + al[i, rows, :] * mid

    def step_row(src, write, i, y, size):
        _, out, held = fine_row(src, i, y, size)
        write(i, y, size, out)
        sv[i, pl.ds(y, size), :] = held

    def write_a(i, y, size, out):
        ma[i + 1, pl.ds(y + PAD, size), :] = out

    def write_b(i, y, size, out):
        mb[i + 1, pl.ds(y + PAD, size), :] = out

    def write_end(i, y, size, out):
        ends[0, i, pl.ds(y, size), :] = out

    def attach_edge(i):
        old = sv[i]
        sv[i] = (old - be[i] * old) + al[i] * ma[i + 1, pl.ds(PAD, SIDE), :]

    def edge_copies(k, c):
        rows = pl.ds(c * WIDE, WIDE)
        out = []
        for way, (to, sends, receives) in enumerate(((up, has_up, has_dn), (dn, has_dn, has_up))):
            for lay in range(2):
                out.append((sends, receives, remote(
                    snd.at[way, lay, rows], hal.at[k, way, lay, rows],
                    snd_sem.at[k, way, lay, c], hal_sem.at[k, way, lay, c], to,
                )))
        return out

    def send_edges(k, c):
        y = pl.multiple_of(c * WIDE, WIDE)
        rows = pl.ds(y, WIDE)
        for way, i, coef in ((0, ROWS - 1, p1), (1, 0, n1)):
            mid, out, _ = fine_row(ma, i, y, WIDE)
            mb[i + 1, pl.ds(y + PAD, WIDE), :] = out
            factor = coef[i + 1, rows, :]
            snd[way, 0, rows, :] = factor * mid
            snd[way, 1, rows, :] = factor * out
        for sends, _, copy in edge_copies(k, c):
            pl.when(sends)(copy.start)

    def take_edges(k, c):
        for _, receives, copy in edge_copies(k, c):
            pl.when(receives)(copy.wait_recv)

        y = pl.multiple_of(c * WIDE, WIDE)
        rows = pl.ds(y, WIDE)
        padded = pl.ds(y + PAD, WIDE)
        mb[1, padded, :] = mb[1, padded, :] + hal[k, 0, 0, rows, :]
        mb[ROWS, padded, :] = mb[ROWS, padded, :] + hal[k, 1, 0, rows, :]
        mb[0, padded, :] = hal[k, 0, 1, rows, :] + st[0, rows, :] * snd[1, 0, rows, :]
        mb[ROWS + 1, padded, :] = hal[k, 1, 1, rows, :] + st[1, rows, :] * snd[0, 0, rows, :]

    def edge_step(write, c):
        y = pl.multiple_of(c * WIDE, WIDE)
        for i in (0, ROWS - 1, 1, ROWS - 2):
            step_row(mb, write, i, y, WIDE)

    def wait_edges(k, c):
        for sends, _, copy in edge_copies(k, c):
            pl.when(sends)(copy.wait_send)

    def ready(k):
        for copy in loads(order(k)):
            copy.wait()
        start_loads(k + 4)

    each(4, ready)
    restrict_shifted(0, CROWS - 1)
    each(4, lambda k: fine_coefs(order(k)))
    each(4, lambda k: start_loads(k + 8))

    pl.semaphore_wait(barrier, 3 + has_up.astype(jnp.int32) + has_dn.astype(jnp.int32))

    own_half = pl.ds(core * HALF, HALF)
    other_half = pl.ds((1 - core) * HALF, HALF)
    st_up = remote(p1.at[ROWS, own_half], st.at[0, own_half], st_snd.at[0], st_rcv.at[0], up)
    st_dn = remote(n1.at[1, own_half], st.at[1, own_half], st_snd.at[1], st_rcv.at[1], dn)
    pl.when(has_up)(st_up.start)
    pl.when(has_dn)(st_dn.start)

    each(CHUNKS, lambda c: send_edges(0, c))

    def later(n):
        pairs = (n + 1, CROWS - 2 - n)
        for j in pairs:
            for b in range(2):
                for copy in loads(2 * j + b):
                    copy.wait()
        restrict_shifted(*pairs)
        for j in pairs:
            for b in range(2):
                fine_coefs(2 * j + b)

    each(2, later)

    inner = pl.ds(PAD, SIDE)

    def restrict_start(n):
        items = []
        for j in (2 * n, 2 * n + 1):
            items.append((lambda b, j=j: ma[2 * j + b + 1, inner, :], put(rs_own, 0, j)))
            items.append((lambda b, j=j: sv[2 * j + b], put(rs_own, 1, j)))
        restrict_pairs(items)

    each(CROWS // 2, restrict_start)

    rs_copy = remote(rs_own, rs_next, rs_sem.at[0], rs_sem.at[1], sibling)
    pl.when(t > 0)(rs_copy.start)

    @pl.when(t == 1)
    def _():
        for comp in range(2):
            for j in range(CROWS):
                rs_next[comp, j] = jnp.zeros((HALF, HALF), F32)

    attach_edge(0)
    attach_edge(ROWS - 1)
    each(ROWS - 2, lambda n: step_row(ma, write_b, n + 1, 0, SIDE), unroll=2)

    fw = [remote(st.at[w, own_half], st.at[w, own_half], fw_snd.at[w], fw_rcv.at[w], sibling) for w in range(2)]
    fr = [remote(st.at[w, other_half], st.at[w, other_half], fw_snd.at[w], fw_rcv.at[w], sibling) for w in range(2)]
    for w, exists, copy in ((0, has_dn, st_up), (1, has_up, st_dn)):
        @pl.when(exists)
        def _(w=w, copy=copy):
            copy.wait_recv()
            fw[w].start()
    for w, exists in ((0, has_dn), (1, has_up)):
        pl.when(exists)(fr[w].wait_recv)

    def restrict_static(j):
        restrict_pairs((
            (lambda b: p1[2 * j + b + 1] - n1[2 * j + b + 1], put(pc1, j + 1)),
            (lambda b: 2.0 * al[2 * j + b], put(alc, j)),
            (lambda b: 2.0 * be[2 * j + b], put(bec, j)),
        ))

    crow = iota((HALF, HALF), 0)
    clane = iota((HALF, HALF), 1)
    coarse_spread = 0.5 * SPREAD

    def coarse_coefs(j):
        u1, u2, u3 = pc1[j + 1], pc2[j], pc3[j]
        plus1 = jnp.maximum(u1, 0.0) + coarse_spread
        minus1 = plus1 - u1
        plus2 = jnp.maximum(u2, 0.0) + coarse_spread
        minus2 = plus2 - u2
        plus3 = jnp.maximum(u3, 0.0) + coarse_spread
        minus3 = plus3 - u3
        ccc[j] = (1.0 - (plus1 + minus1 + plus2 + minus2 + plus3 + minus3)) - alc[j]
        pc1[j + 1] = plus1
        nc1[j + 1] = minus1
        pc2[j] = jnp.where(crow == 0, 0.0, pltpu.roll(plus2, 1, 0))
        nc2[j] = jnp.where(crow == HALF - 1, 0.0, pltpu.roll(minus2, HALF - 1, 0))
        pc3[j] = jnp.where(clane == 0, 0.0, pltpu.roll(plus3, 1, 1))
        nc3[j] = jnp.where(clane == HALF - 1, 0.0, pltpu.roll(minus3, HALF - 1, 1))

    is_last = t == LAST
    runs = t % 2 == 1
    cst_up = remote(pc1.at[CROWS], cst.at[0], cst_snd.at[0], cst_rcv.at[0], up)
    cst_dn = remote(nc1.at[1], cst.at[1], cst_snd.at[1], cst_rcv.at[1], dn)

    def d_pieces(group, comp):
        if group == 0:
            return ((comp, pl.ds(2, 2)),)
        first = 2 - group
        return ((4 * group - 2 + comp, pl.ds(first, 1)), (4 * group + comp, pl.ds(CROWS - 1 - first, 1)))

    def d_copies(*groups, to=LAST):
        return [
            remote(
                d_own.at[comp, rows], dd.at[t, comp, rows],
                d_snd.at[0 if to == LAST else 1, n], d_rcv.at[t, n], {"tm": to},
            )
            for group in groups for comp in range(2) for n, rows in d_pieces(group, comp)
        ]

    def send_jump(*groups):
        for copy in d_copies(*groups):
            copy.start()

        @pl.when(t == 0)
        def _():
            for copy in d_copies(*groups, to=1):
                copy.start()

    keep = jnp.where(t == 1, 0.0, 1.0)

    def jump(*rows):
        def item(comp, j):
            def write(value):
                d_own[comp, j] = value - keep * rs_next[comp, j]
            return lambda b: ends[comp, 2 * j + b], write

        restrict_pairs([item(comp, j) for j in rows for comp in range(2)])

    def fill(n):
        def two(write, src, first):
            for b in range(2):
                step_row(src, write, first + b, 0, SIDE)

        pl.when(n < 4)(lambda: two(write_a, mb, 2 + 2 * n))
        pl.when(jnp.logical_and(n >= 4, n < 7))(lambda: two(write_b, ma, 3 + 2 * (n - 4)))
        pl.when(jnp.logical_and(n >= 7, n < 9))(lambda: two(write_end, mb, 4 + 2 * (n - 7)))

        @pl.when(jnp.logical_and(runs, n >= 4))
        def _():
            restrict_static(n - 4)
            coarse_coefs(n - 4)

        @pl.when(jnp.logical_and(jnp.logical_not(is_last), n == 9))
        def _():
            pl.when(t != 1)(rs_copy.wait_recv)
            jump(2, 3)
            send_jump(0)

    def between(n):
        pl.when(n < CHUNKS)(lambda: take_edges(0, n))
        pl.when(jnp.logical_and(n >= 1, n <= CHUNKS))(lambda: edge_step(write_a, n - 1))

        @pl.when(n >= 2)
        def _():
            wait_edges(0, n - 2)
            send_edges(1, n - 2)

        fill(n)

    each(CHUNKS + 2, between)

    attach_edge(0)
    attach_edge(ROWS - 1)
    for i in (1, 2, ROWS - 3, ROWS - 2):
        step_row(ma, write_b, i, 0, SIDE)
    for i in (2, 3, ROWS - 4, ROWS - 3):
        step_row(mb, write_end, i, 0, SIDE)

    @pl.when(jnp.logical_not(is_last))
    def _():
        jump(1, 4)

        pl.when(t != 1)(lambda: send_jump(1))

    @pl.when(runs)
    def _():
        pl.when(has_up)(cst_up.start)
        pl.when(has_dn)(cst_dn.start)
        zero = jnp.zeros((HALF, HALF), F32)
        one = jnp.ones((HALF, HALF), F32)
        pc1[0] = one
        nc1[CROWS + 1] = one
        margin = jnp.zeros((PAD, HALF), F32)
        middle = pl.ds(PAD, HALF)

        def margins(j):
            for ref in (mca, mcb):
                ref[j, pl.ds(0, PAD), :] = margin
                ref[j, pl.ds(PAD + HALF, PAD), :] = margin

        each(CROWS + 2, margins)
        for j in (0, CROWS + 1):
            mca[j, middle, :] = zero

        @pl.when(jnp.logical_not(has_dn))
        def _():
            cst[0] = zero
            for k in range(3):
                for lay in range(2):
                    chal[k, 0, lay] = zero

        @pl.when(jnp.logical_not(has_up))
        def _():
            cst[1] = zero
            for k in range(3):
                for lay in range(2):
                    chal[k, 1, lay] = zero

    def finish(n):
        pl.when(n < CHUNKS)(lambda: take_edges(1, n))
        pl.when(n >= 1)(lambda: edge_step(write_end, n - 1))

    each(CHUNKS + 1, finish)

    @pl.when(jnp.logical_not(is_last))
    def _():
        jump(0, CROWS - 1)

        @pl.when(t == 1)
        def _():
            pl.semaphore_wait(turn_sem, 1)
            for copy in d_copies(1):
                copy.start()

        send_jump(2)

        @pl.when(t == 0)
        def _():
            for copy in d_copies(2):
                copy.wait_send()
            pl.semaphore_signal(turn_sem, inc=1, device_id={"tm": 1}, device_id_type=MESH)

    middle = pl.ds(PAD, HALF)

    def coarse_row(src, j):
        wide = src[j + 1]
        mid = wide[PAD:PAD + HALF]
        old = sc[j]
        off = bec[j] * old
        out = ccc[j] * mid + off
        out = out + (pc1[j] * src[j, middle, :] + nc1[j + 2] * src[j + 2, middle, :])
        out = out + (pc2[j] * wide[PAD - 1:PAD - 1 + HALF] + nc2[j] * wide[PAD + 1:PAD + 1 + HALF])
        out = out + (pc3[j] * pltpu.roll(mid, 1, 1) + nc3[j] * pltpu.roll(mid, HALF - 1, 1))
        return mid, out, (old - off) + alc[j] * mid

    def coarse_second(turn, *rows):
        for j in rows:
            _, out, held = coarse_row(mcb, j)
            dd[turn - 1, 0, j] = out
            dd[turn - 1, 1, j] = held

    def coarse_edge_copies(turn):
        out = []
        for way, (to, sends, receives) in enumerate(((up, has_up, has_dn), (dn, has_dn, has_up))):
            for lay in range(2):
                out.append((sends, receives, remote(
                    csnd.at[way, lay], chal.at[turn - 1, way, lay],
                    c_snd.at[turn - 1, way, lay], c_rcv.at[turn - 1, way, lay], to,
                )))
        return out

    g_copy = remote(dd.at[1], g_in, g_sem.at[0], g_sem.at[1], {"tm": 2})

    def chain(turn):
        for group, comp in ((0, 0), (0, 1), (1, 0), (1, 1), (2, 0), (2, 1)):
            for n, rows in d_pieces(group, comp):
                remote(
                    d_own.at[comp, rows], dd.at[turn - 1, comp, rows],
                    d_snd.at[0, n], d_rcv.at[turn - 1, n], {"tm": 0},
                ).wait_recv()

        taken = jnp.where(turn == 2, 1.0, 0.0)
        pl.when(turn == 2)(rs_copy.wait_recv)

        @pl.when(turn == 1)
        def _():
            for j in range(CROWS):
                mca[j + 1, middle, :] = dd[0, 0, j]
                sc[j] = dd[0, 1, j]

        @pl.when(turn > 1)
        def _():
            for j in range(CROWS):
                mca[j + 1, middle, :] = (dd[turn - 1, 0, j] - taken * rs_next[0, j]) + dd[turn - 2, 0, j]
                sc[j] = (dd[turn - 1, 1, j] - taken * rs_next[1, j]) + dd[turn - 2, 1, j]

        @pl.when(turn > 1)
        def _():
            for sends, _, copy in coarse_edge_copies(turn - 1):
                pl.when(sends)(copy.wait_send)

        for way, j, coef in ((0, CROWS - 1, pc1), (1, 0, nc1)):
            mid, out, _ = coarse_row(mca, j)
            mcb[j + 1, middle, :] = out
            factor = coef[j + 1]
            csnd[way, 0] = factor * mid
            csnd[way, 1] = factor * out
        for sends, _, copy in coarse_edge_copies(turn):
            pl.when(sends)(copy.start)

        for j in (0, CROWS - 1):
            old = sc[j]
            sc[j] = (old - bec[j] * old) + alc[j] * mca[j + 1, middle, :]
        for j in range(1, CROWS - 1):
            _, out, held = coarse_row(mca, j)
            mcb[j + 1, middle, :] = out
            sc[j] = held
        coarse_second(turn, *range(2, CROWS - 2))

        @pl.when(turn == 1)
        def _():
            pl.when(has_dn)(cst_up.wait_recv)
            pl.when(has_up)(cst_dn.wait_recv)

        for _, receives, copy in coarse_edge_copies(turn):
            pl.when(receives)(copy.wait_recv)
        mcb[1, middle, :] = mcb[1, middle, :] + chal[turn - 1, 0, 0]
        mcb[CROWS, middle, :] = mcb[CROWS, middle, :] + chal[turn - 1, 1, 0]
        mcb[0, middle, :] = chal[turn - 1, 0, 1] + cst[0] * csnd[1, 0]
        mcb[CROWS + 1, middle, :] = chal[turn - 1, 1, 1] + cst[1] * csnd[0, 0]
        coarse_second(turn, 0, CROWS - 1, 1, CROWS - 2)

        pl.when(turn == 2)(g_copy.start)

    @pl.when(runs)
    def _():
        turns = jnp.where(is_last, LAST, 1)
        each(turns, lambda n: chain(n + 1))

        def result(j):
            g_out[0, j] = dd[turns - 1, 0, j]
            g_out[1, j] = dd[turns - 1, 1, j]

        each(CROWS, result)
        pl.when(is_last)(g_copy.wait_send)
        for sends, _, copy in coarse_edge_copies(turns):
            pl.when(sends)(copy.wait_send)
        pl.when(has_up)(cst_up.wait_send)
        pl.when(has_dn)(cst_dn.wait_send)

    @pl.when(t == 2)
    def _():
        g_copy.wait_recv()

        def result(j):
            g_out[0, j] = g_in[0, j]
            g_out[1, j] = g_in[1, j]

        each(CROWS, result)

    @pl.when(t == 0)
    def _():
        def result(j):
            g_out[0, j] = jnp.zeros((HALF, HALF), F32)
            g_out[1, j] = jnp.zeros((HALF, HALF), F32)

        each(CROWS, result)
        for copy in d_copies(0, 1) + d_copies(0, 1, 2, to=1):
            copy.wait_send()

    @pl.when(jnp.logical_or(t == 1, t == 2))
    def _():
        for copy in d_copies(0, 1, 2):
            copy.wait_send()

    each(CHUNKS, lambda c: wait_edges(1, c))
    pl.when(has_up)(st_up.wait_send)
    pl.when(has_dn)(st_dn.wait_send)
    pl.when(has_dn)(fw[0].wait_send)
    pl.when(has_up)(fw[1].wait_send)
    pl.when(t > 0)(rs_copy.wait_send)


def final_kernel(ends, g, out, buf, sem):
    wide = (iota((HALF, SIDE), 0) == (iota((HALF, SIDE), 1) // 2)).astype(F32).astype(BF16)
    tall = ((iota((SIDE, HALF), 0) // 2) == iota((SIDE, HALF), 1)).astype(F32).astype(BF16)

    def copy(comp, i):
        return pltpu.make_async_copy(buf.at[comp, i], out.at[comp, i], sem.at[comp, i])

    def body(n):
        comp, j = n // CROWS, n % CROWS
        spread = None
        for part in split(g[comp, j]):
            term = dot(tall, dot(part, wide).astype(BF16))
            spread = term if spread is None else spread + term
        for b in range(2):
            buf[comp, 2 * j + b] = ends[comp, 2 * j + b] + spread
            copy(comp, 2 * j + b).start()

    each(2 * CROWS, body, unroll=2)
    each(2 * ROWS, lambda n: copy(n // ROWS, n % ROWS).wait())


def per_device(start_states, velocity, site_class, attach_rates, detach_rates):
    any_ref = pl.BlockSpec(memory_space=pl.ANY)
    smem = pl.BlockSpec(memory_space=pltpu.SMEM)
    vmem = pl.BlockSpec(memory_space=pltpu.VMEM)
    start = start_states.reshape(start_states.shape[1:])
    plane = (SIDE, SIDE)
    cplane = (HALF, HALF)
    coarse = (2, CROWS) + cplane

    def buf(*shape):
        return pltpu.VMEM(shape, F32)

    brick = buf(ROWS, *plane)
    cbrick = buf(CROWS, *cplane)
    dma = pltpu.SemaphoreType.DMA
    ends, g = pl.pallas_call(
        main_kernel,
        out_shape=(pltpu.VMEM((2, ROWS) + plane, F32), pltpu.VMEM(coarse, F32)),
        in_specs=[any_ref, any_ref, any_ref, smem, smem],
        out_specs=(vmem, vmem),
        scratch_shapes=[
            buf(ROWS + 2, SIDE + 2 * PAD, SIDE), buf(ROWS + 2, SIDE + 2 * PAD, SIDE),
            buf(ROWS + 2, *plane), buf(ROWS + 2, *plane), brick, brick, brick, brick, brick, brick, brick,
            pltpu.VMEM((8,) + plane, jnp.int32),
            buf(2, 2, *plane), buf(2, 2, 2, *plane), buf(2, *plane),
            buf(*coarse), buf(*coarse), buf(*coarse), buf(3, *coarse), buf(*coarse),
            buf(CROWS + 2, HALF + 2 * PAD, HALF), buf(CROWS + 2, HALF + 2 * PAD, HALF), cbrick,
            buf(CROWS + 2, *cplane), buf(CROWS + 2, *cplane), cbrick, cbrick, cbrick, cbrick, cbrick, cbrick, cbrick,
            buf(2, 2, *cplane), buf(3, 2, 2, *cplane), buf(2, *cplane), buf(PLANES, SIDE, HALF),
            dma((6, ROWS)), dma((2, 2, 2, CHUNKS)), dma((2, 2, 2, CHUNKS)), dma((2,)), dma((2,)), dma((2,)), dma((2,)),
            dma((2,)), pltpu.SemaphoreType.REGULAR, dma((2, 10)), dma((3, 10)), dma((2,)), dma((3, 2, 2)), dma((3, 2, 2)), dma((2,)), dma((2,)),
        ],
        compiler_params=pltpu.CompilerParams(
            collective_id=0, has_side_effects=True, vmem_limit_bytes=56 * 1024 * 1024
        ),
    )(start, velocity, site_class, attach_rates, detach_rates)
    out = pl.pallas_call(
        final_kernel,
        out_shape=jax.ShapeDtypeStruct((2, ROWS) + plane, F32),
        in_specs=[vmem, vmem],
        out_specs=any_ref,
        scratch_shapes=[buf(2, ROWS, *plane), dma((2, ROWS))],
        compiler_params=pltpu.CompilerParams(vmem_limit_bytes=40 * 1024 * 1024),
    )(ends, g)
    return out[None]


def solution(mesh):
    in_specs = (
        P("tm", None, "space", None, None),
        P(None, "space", None, None),
        P("space", None, None),
        P(),
        P(),
    )
    return jax.shard_map(
        per_device, mesh=mesh, in_specs=in_specs, out_specs=P("tm", None, "space", None, None), check_vma=False
    )
```

```python
import jax
import jax.numpy as jnp
from jax import lax
from jax.experimental import pallas as pl
from jax.experimental.pallas import tpu as pltpu
from jax.sharding import PartitionSpec as P

MESH = pl.DeviceIdType.MESH
F32 = jnp.float32
BF16 = jnp.bfloat16

ROWS = 12
SIDE = 256
HALF = SIDE // 2
CROWS = ROWS // 2
PAD = 8
CHUNKS = 8
WIDE = SIDE // CHUNKS
SUB = 32
COEF = 128
PLANES = 4
SPREAD = 0.08
LAST = 3


def iota(shape, axis):
    return lax.broadcasted_iota(jnp.int32, shape, axis)


def pair_columns(scale):
    match = (iota((SIDE, HALF), 0) // 2) == iota((SIDE, HALF), 1)
    return jnp.where(match, scale, 0.0).astype(BF16)


def split(values):
    high = values.astype(BF16)
    return high, (values - high.astype(F32)).astype(BF16)


def dot(left, right):
    return jnp.dot(left, right, preferred_element_type=F32)


def each(count, body, unroll=1):
    lax.fori_loop(0, count, lambda i, _: (body(i), 0)[1], 0, unroll=unroll)


def main_kernel(
    start, velocity, site_class, attach_table, detach_table,
    ends, g_out,
    ma, mb, p1, n1, p2, n2, p3, n3, cc, al, be, cls,
    snd, hal, st,
    rs_own, rs_next, d_own, dd, g_in,
    mca, mcb, sc, pc1, nc1, pc2, nc2, pc3, nc3, ccc, alc, bec,
    csnd, chal, cst, tmp,
    load_sem, snd_sem, hal_sem, st_snd, st_rcv, fw_snd, fw_rcv,
    rs_sem, turn_sem, d_snd, d_rcv, g_sem, c_snd, c_rcv, cst_snd, cst_rcv,
):
    t = lax.axis_index("tm")
    s = lax.axis_index("space")
    has_up = s < 31
    has_dn = s > 0
    up = {"space": jnp.minimum(s + 1, 31)}
    dn = {"space": jnp.maximum(s - 1, 0)}
    core = t % 2
    sibling = {"tm": t + 1 - 2 * core}

    def remote(src, dst, send, recv, to):
        return pltpu.make_async_remote_copy(
            src_ref=src, dst_ref=dst, send_sem=send, recv_sem=recv,
            device_id=to, device_id_type=MESH,
        )

    barrier = pltpu.get_barrier_semaphore()
    for j in (1, 2, 3):
        pl.semaphore_signal(barrier, inc=1, device_id={"tm": (t + j) % 4}, device_id_type=MESH)

    @pl.when(has_up)
    def _():
        pl.semaphore_signal(barrier, inc=1, device_id=up, device_id_type=MESH)

    @pl.when(has_dn)
    def _():
        pl.semaphore_signal(barrier, inc=1, device_id=dn, device_id_type=MESH)

    def loads(i):
        inner = pl.ds(PAD, SIDE)
        pairs = (
            (velocity.at[0, i], p1.at[i + 1]),
            (velocity.at[1, i], p2.at[i]),
            (velocity.at[2, i], p3.at[i]),
            (site_class.at[i], cls.at[slot(i)]),
            (start.at[0, i], ma.at[i + 1, inner]),
            (start.at[1, i], ends.at[1, i]),
        )
        return [pltpu.make_async_copy(a, b, load_sem.at[j, i]) for j, (a, b) in enumerate(pairs)]

    def slot(i):
        return jnp.where(i < CROWS, 2 * i, 2 * (ROWS - 1 - i) + 1) % 8

    def order(k):
        return jnp.where(k % 2 == 0, k // 2, ROWS - 1 - k // 2)

    def start_loads(k):
        for copy in loads(order(k)):
            copy.start()

    each(4, start_loads)

    blank = jnp.zeros((PAD, SIDE), F32)

    def clear(i):
        for ref in (ma, mb):
            ref[i, pl.ds(0, PAD), :] = blank
            ref[i, pl.ds(PAD + SIDE, PAD), :] = blank

    each(ROWS + 2, clear)

    def clear_rows(c):
        rows = pl.ds(PAD + c * SUB, SUB)
        plain = pl.ds(c * SUB, SUB)
        zero = jnp.zeros((SUB, SIDE), F32)
        one = jnp.ones((SUB, SIDE), F32)
        for ref in (ma, mb):
            ref[0, rows, :] = zero
            ref[ROWS + 1, rows, :] = zero
        p1[0, plain, :] = one
        n1[ROWS + 1, plain, :] = one

        @pl.when(jnp.logical_not(has_dn))
        def _():
            st[0, plain, :] = zero
            for k in range(2):
                for lay in range(2):
                    hal[k, 0, lay, plain, :] = zero

        @pl.when(jnp.logical_not(has_up))
        def _():
            st[1, plain, :] = zero
            for k in range(2):
                for lay in range(2):
                    hal[k, 1, lay, plain, :] = zero

    each(SIDE // SUB, clear_rows)

    columns_table = pair_columns(0.125)

    def restrict_pairs(items):
        for n, (read, _) in enumerate(items):
            high, low = split(read(0) + read(1))
            tmp[n] = dot(high, columns_table) + dot(low, columns_table)
        for n, (_, write) in enumerate(items):
            write(tmp[n, pl.ds(0, HALF, 2), :] + tmp[n, pl.ds(1, HALF, 2), :])

    def put(ref, *index):
        def write(value):
            ref[index] = value
        return write

    def restrict_shifted(*pairs):
        items = []
        for j in pairs:
            items.append((lambda b, j=j: p2[2 * j + b], put(pc2, j)))
            items.append((lambda b, j=j: p3[2 * j + b], put(pc3, j)))
        restrict_pairs(items)

    row8 = iota((COEF, SIDE), 0)
    lane = iota((COEF, SIDE), 1)

    def fine_coefs(i):
        def body(c, before):
            y = pl.multiple_of(c * COEF, COEF)
            rows = pl.ds(y, COEF)
            u1 = p1[i + 1, rows, :]
            u2 = p2[i, rows, :]
            u3 = p3[i, rows, :]
            after = p2[i, pl.ds(pl.multiple_of(jnp.minimum(y + COEF, SIDE - PAD), PAD), PAD), :]
            wide = jnp.concatenate([before, u2, after], axis=0)
            wide_plus = jnp.maximum(wide, 0.0) + SPREAD
            wide_minus = wide_plus - wide
            plus1 = jnp.maximum(u1, 0.0) + SPREAD
            minus1 = plus1 - u1
            plus3 = jnp.maximum(u3, 0.0) + SPREAD
            minus3 = plus3 - u3
            kind = cls[slot(i), rows, :]
            attach = jnp.zeros((COEF, SIDE), F32)
            detach = jnp.zeros((COEF, SIDE), F32)
            for level in range(8):
                here = kind == level
                attach = jnp.where(here, attach_table[level], attach)
                detach = jnp.where(here, detach_table[level], detach)
            total = plus1 + minus1 + wide_plus[PAD:PAD + COEF] + wide_minus[PAD:PAD + COEF] + plus3 + minus3
            p1[i + 1, rows, :] = plus1
            n1[i + 1, rows, :] = minus1
            p2[i, rows, :] = jnp.where(row8 + y == 0, 0.0, wide_plus[PAD - 1:PAD - 1 + COEF])
            n2[i, rows, :] = jnp.where(row8 + y == SIDE - 1, 0.0, wide_minus[PAD + 1:PAD + 1 + COEF])
            p3[i, rows, :] = jnp.where(lane == 0, 0.0, pltpu.roll(plus3, 1, 1))
            n3[i, rows, :] = jnp.where(lane == SIDE - 1, 0.0, pltpu.roll(minus3, SIDE - 1, 1))
            cc[i, rows, :] = (1.0 - total) - attach
            al[i, rows, :] = attach
            be[i, rows, :] = detach
            return u2[COEF - PAD:]

        lax.fori_loop(0, SIDE // COEF, body, jnp.zeros((PAD, SIDE), F32), unroll=SIDE // COEF)

    sv = ends.at[1]

    def fine_row(src, i, y, size):
        rows = pl.ds(y, size)
        wide = src[i + 1, pl.ds(y, size + 2 * PAD), :]
        mid = wide[PAD:PAD + size]
        old = sv[i, rows, :]
        off = be[i, rows, :] * old
        padded = pl.ds(y + PAD, size)
        out = cc[i, rows, :] * mid + off
        out = out + (p1[i, rows, :] * src[i, padded, :] + n1[i + 2, rows, :] * src[i + 2, padded, :])
        out = out + (p2[i, rows, :] * wide[PAD - 1:PAD - 1 + size] + n2[i, rows, :] * wide[PAD + 1:PAD + 1 + size])
        out = out + (p3[i, rows, :] * pltpu.roll(mid, 1, 1) + n3[i, rows, :] * pltpu.roll(mid, SIDE - 1, 1))
        return mid, out, (old - off) + al[i, rows, :] * mid

    def step_row(src, write, i, y, size):
        _, out, held = fine_row(src, i, y, size)
        write(i, y, size, out)
        sv[i, pl.ds(y, size), :] = held

    def write_a(i, y, size, out):
        ma[i + 1, pl.ds(y + PAD, size), :] = out

    def write_b(i, y, size, out):
        mb[i + 1, pl.ds(y + PAD, size), :] = out

    def write_end(i, y, size, out):
        ends[0, i, pl.ds(y, size), :] = out

    def attach_edge(i):
        old = sv[i]
        sv[i] = (old - be[i] * old) + al[i] * ma[i + 1, pl.ds(PAD, SIDE), :]

    def edge_copies(k, c):
        rows = pl.ds(c * WIDE, WIDE)
        out = []
        for way, (to, sends, receives) in enumerate(((up, has_up, has_dn), (dn, has_dn, has_up))):
            for lay in range(2):
                out.append((sends, receives, remote(
                    snd.at[way, lay, rows], hal.at[k, way, lay, rows],
                    snd_sem.at[k, way, lay, c], hal_sem.at[k, way, lay, c], to,
                )))
        return out

    def send_edges(k, c):
        y = pl.multiple_of(c * WIDE, WIDE)
        rows = pl.ds(y, WIDE)
        for way, i, coef in ((0, ROWS - 1, p1), (1, 0, n1)):
            mid, out, _ = fine_row(ma, i, y, WIDE)
            mb[i + 1, pl.ds(y + PAD, WIDE), :] = out
            factor = coef[i + 1, rows, :]
            snd[way, 0, rows, :] = factor * mid
            snd[way, 1, rows, :] = factor * out
        for sends, _, copy in edge_copies(k, c):
            pl.when(sends)(copy.start)

    def take_edges(k, c):
        for _, receives, copy in edge_copies(k, c):
            pl.when(receives)(copy.wait_recv)

        y = pl.multiple_of(c * WIDE, WIDE)
        rows = pl.ds(y, WIDE)
        padded = pl.ds(y + PAD, WIDE)
        mb[1, padded, :] = mb[1, padded, :] + hal[k, 0, 0, rows, :]
        mb[ROWS, padded, :] = mb[ROWS, padded, :] + hal[k, 1, 0, rows, :]
        mb[0, padded, :] = hal[k, 0, 1, rows, :] + st[0, rows, :] * snd[1, 0, rows, :]
        mb[ROWS + 1, padded, :] = hal[k, 1, 1, rows, :] + st[1, rows, :] * snd[0, 0, rows, :]

    def edge_step(write, c):
        y = pl.multiple_of(c * WIDE, WIDE)
        for i in (0, ROWS - 1, 1, ROWS - 2):
            step_row(mb, write, i, y, WIDE)

    def wait_edges(k, c):
        for sends, _, copy in edge_copies(k, c):
            pl.when(sends)(copy.wait_send)

    def start_kinds(k):
        i = order(k + 8)
        pltpu.make_async_copy(site_class.at[i], cls.at[slot(i)], load_sem.at[3, i]).start()

    def ready(k):
        for copy in loads(order(k)):
            copy.wait()
        start_loads(k + 4)
        for n, copy in enumerate(loads(order(k + 8))):
            if n != 3:
                copy.start()

    each(4, ready)
    restrict_shifted(0, CROWS - 1)
    each(4, lambda k: fine_coefs(order(k)))
    each(4, start_kinds)

    pl.semaphore_wait(barrier, 3 + has_up.astype(jnp.int32) + has_dn.astype(jnp.int32))

    own_half = pl.ds(core * HALF, HALF)
    other_half = pl.ds((1 - core) * HALF, HALF)
    st_up = remote(p1.at[ROWS, own_half], st.at[0, own_half], st_snd.at[0], st_rcv.at[0], up)
    st_dn = remote(n1.at[1, own_half], st.at[1, own_half], st_snd.at[1], st_rcv.at[1], dn)
    pl.when(has_up)(st_up.start)
    pl.when(has_dn)(st_dn.start)

    each(CHUNKS, lambda c: send_edges(0, c))

    def more_coefs(p):
        def row(n):
            return jnp.where(n < 2, 2 * p, 2 * (CROWS - 1 - p) - 2) + n

        def arrived(n):
            for copy in loads(row(n))[:4]:
                copy.wait()

        each(4, arrived)
        restrict_shifted(p, CROWS - 1 - p)
        each(4, lambda n: fine_coefs(row(n)))

    def state_arrived(k):
        for copy in loads(order(k + 4))[4:]:
            copy.wait()

    each(ROWS - 4, state_arrived)

    inner = pl.ds(PAD, SIDE)

    def restrict_start(n):
        items = []
        for j in (2 * n, 2 * n + 1):
            items.append((lambda b, j=j: ma[2 * j + b + 1, inner, :], put(rs_own, 0, j)))
            items.append((lambda b, j=j: sv[2 * j + b], put(rs_own, 1, j)))
        restrict_pairs(items)

    each(CROWS // 2, restrict_start)

    rs_copy = remote(rs_own, rs_next, rs_sem.at[0], rs_sem.at[1], sibling)
    @pl.when(t == 1)
    def _():
        for comp in range(2):
            for j in range(CROWS):
                rs_next[comp, j] = jnp.zeros((HALF, HALF), F32)

    pl.when(t > 0)(rs_copy.start)

    fw = [remote(st.at[w, own_half], st.at[w, own_half], fw_snd.at[w], fw_rcv.at[w], sibling) for w in range(2)]
    fr = [remote(st.at[w, other_half], st.at[w, other_half], fw_snd.at[w], fw_rcv.at[w], sibling) for w in range(2)]
    def share_static():
        for w, exists, copy in ((0, has_dn, st_up), (1, has_up, st_dn)):
            @pl.when(exists)
            def _(w=w, copy=copy):
                copy.wait_recv()
                fw[w].start()
        for w, exists in ((0, has_dn), (1, has_up)):
            pl.when(exists)(fr[w].wait_recv)

    def restrict_static(j):
        restrict_pairs((
            (lambda b: p1[2 * j + b + 1] - n1[2 * j + b + 1], put(pc1, j + 1)),
            (lambda b: 2.0 * al[2 * j + b], put(alc, j)),
            (lambda b: 2.0 * be[2 * j + b], put(bec, j)),
        ))

    crow = iota((HALF, HALF), 0)
    clane = iota((HALF, HALF), 1)
    coarse_spread = 0.5 * SPREAD

    def coarse_coefs(j):
        u1, u2, u3 = pc1[j + 1], pc2[j], pc3[j]
        plus1 = jnp.maximum(u1, 0.0) + coarse_spread
        minus1 = plus1 - u1
        plus2 = jnp.maximum(u2, 0.0) + coarse_spread
        minus2 = plus2 - u2
        plus3 = jnp.maximum(u3, 0.0) + coarse_spread
        minus3 = plus3 - u3
        ccc[j] = (1.0 - (plus1 + minus1 + plus2 + minus2 + plus3 + minus3)) - alc[j]
        pc1[j + 1] = plus1
        nc1[j + 1] = minus1
        pc2[j] = jnp.where(crow == 0, 0.0, pltpu.roll(plus2, 1, 0))
        nc2[j] = jnp.where(crow == HALF - 1, 0.0, pltpu.roll(minus2, HALF - 1, 0))
        pc3[j] = jnp.where(clane == 0, 0.0, pltpu.roll(plus3, 1, 1))
        nc3[j] = jnp.where(clane == HALF - 1, 0.0, pltpu.roll(minus3, HALF - 1, 1))

    is_last = t == LAST
    runs = t % 2 == 1
    cst_up = remote(pc1.at[CROWS], cst.at[0], cst_snd.at[0], cst_rcv.at[0], up)
    cst_dn = remote(nc1.at[1], cst.at[1], cst_snd.at[1], cst_rcv.at[1], dn)

    def d_pieces(group, comp):
        if group == 0:
            return ((comp, pl.ds(2, 2)),)
        first = 2 - group
        return ((4 * group - 2 + comp, pl.ds(first, 1)), (4 * group + comp, pl.ds(CROWS - 1 - first, 1)))

    def d_copies(*groups, to=LAST):
        return [
            remote(
                d_own.at[comp, rows], dd.at[t, comp, rows],
                d_snd.at[0 if to == LAST else 1, n], d_rcv.at[t, n], {"tm": to},
            )
            for group in groups for comp in range(2) for n, rows in d_pieces(group, comp)
        ]

    def send_jump(*groups):
        for copy in d_copies(*groups):
            copy.start()

        @pl.when(t == 0)
        def _():
            for copy in d_copies(*groups, to=1):
                copy.start()

    keep = jnp.where(t == 1, 0.0, 1.0)

    def jump(*rows):
        def item(comp, j):
            def write(value):
                d_own[comp, j] = value - keep * rs_next[comp, j]
            return lambda b: ends[comp, 2 * j + b], write

        restrict_pairs([item(comp, j) for j in rows for comp in range(2)])

    def among(n, *values):
        found = n == values[0]
        for value in values[1:]:
            found = jnp.logical_or(found, n == value)
        return found

    def fill(n):
        outer = among(n, 1, 11)
        pl.when(among(n, 0, 2))(lambda: more_coefs(jnp.where(n == 0, 1, 2)))
        pl.when(outer)(lambda: (attach_edge(0), attach_edge(ROWS - 1), None)[2])

        @pl.when(among(n, 1, 3, 6, 11))
        def _():
            def body(m):
                first = jnp.where(outer, 1 + (ROWS - 4) * m, 3 + 2 * m)
                for b in range(2):
                    step_row(ma, write_b, first + b, 0, SIDE)

            each(jnp.where(outer, 2, 3), body)

        @pl.when(among(n, 4, 5))
        def _():
            each(4, lambda m: step_row(mb, write_a, 4 * n - 14 + m, 0, SIDE), unroll=2)

        @pl.when(among(n, 7, 11))
        def _():
            def body(m):
                first = jnp.where(outer, 2 + (ROWS - 6) * m, 4 + 2 * m)
                for b in range(2):
                    step_row(mb, write_end, first + b, 0, SIDE)

            each(2, body)

        @pl.when(jnp.logical_and(runs, jnp.logical_and(n >= 4, n < 10)))
        def _():
            restrict_static(n - 4)
            coarse_coefs(n - 4)

        @pl.when(jnp.logical_and(jnp.logical_not(is_last), among(n, 8, 11)))
        def _():
            pl.when(jnp.logical_and(n == 8, t != 1))(rs_copy.wait_recv)
            p = jnp.where(n == 8, 2, 1)
            jump(p, CROWS - 1 - p)
            pl.when(jnp.logical_and(n == 8, t != 1))(lambda: send_jump(0))
            pl.when(jnp.logical_and(n == 11, t != 1))(lambda: send_jump(1))

    def between(n):
        fill(n)
        pl.when(n == 1)(share_static)
        pl.when(jnp.logical_and(n >= 1, n <= CHUNKS))(lambda: take_edges(0, n - 1))
        pl.when(jnp.logical_and(n >= 2, n <= CHUNKS + 1))(lambda: edge_step(write_a, n - 2))

        @pl.when(jnp.logical_and(n >= 3, n <= CHUNKS + 2))
        def _():
            wait_edges(0, n - 3)
            send_edges(1, n - 3)

    each(CHUNKS + 4, between)

    @pl.when(runs)
    def _():
        pl.when(has_up)(cst_up.start)
        pl.when(has_dn)(cst_dn.start)
        zero = jnp.zeros((HALF, HALF), F32)
        one = jnp.ones((HALF, HALF), F32)
        pc1[0] = one
        nc1[CROWS + 1] = one
        margin = jnp.zeros((PAD, HALF), F32)
        middle = pl.ds(PAD, HALF)

        def margins(j):
            for ref in (mca, mcb):
                ref[j, pl.ds(0, PAD), :] = margin
                ref[j, pl.ds(PAD + HALF, PAD), :] = margin

        each(CROWS + 2, margins)
        for j in (0, CROWS + 1):
            mca[j, middle, :] = zero

        @pl.when(jnp.logical_not(has_dn))
        def _():
            cst[0] = zero
            for k in range(3):
                for lay in range(2):
                    chal[k, 0, lay] = zero

        @pl.when(jnp.logical_not(has_up))
        def _():
            cst[1] = zero
            for k in range(3):
                for lay in range(2):
                    chal[k, 1, lay] = zero

    def finish(n):
        pl.when(n < CHUNKS)(lambda: take_edges(1, n))
        pl.when(n >= 1)(lambda: edge_step(write_end, n - 1))

    each(CHUNKS + 1, finish)

    @pl.when(jnp.logical_not(is_last))
    def _():
        jump(0, CROWS - 1)

        @pl.when(t == 1)
        def _():
            pl.semaphore_wait(turn_sem, 1)
            for copy in d_copies(0, 1):
                copy.start()

        send_jump(2)

        @pl.when(t == 0)
        def _():
            first, second, *rest = d_copies(2)
            first.wait_send()
            second.wait_send()
            pl.semaphore_signal(turn_sem, inc=1, device_id={"tm": 1}, device_id_type=MESH)
            for copy in rest:
                copy.wait_send()

    middle = pl.ds(PAD, HALF)

    def coarse_row(src, j):
        wide = src[j + 1]
        mid = wide[PAD:PAD + HALF]
        old = sc[j]
        off = bec[j] * old
        out = ccc[j] * mid + off
        out = out + (pc1[j] * src[j, middle, :] + nc1[j + 2] * src[j + 2, middle, :])
        out = out + (pc2[j] * wide[PAD - 1:PAD - 1 + HALF] + nc2[j] * wide[PAD + 1:PAD + 1 + HALF])
        out = out + (pc3[j] * pltpu.roll(mid, 1, 1) + nc3[j] * pltpu.roll(mid, HALF - 1, 1))
        return mid, out, (old - off) + alc[j] * mid

    def coarse_second(turn, *rows):
        for j in rows:
            _, out, held = coarse_row(mcb, j)
            dd[turn - 1, 0, j] = out
            dd[turn - 1, 1, j] = held

    def coarse_edge_copies(turn):
        out = []
        for way, (to, sends, receives) in enumerate(((up, has_up, has_dn), (dn, has_dn, has_up))):
            for lay in range(2):
                out.append((sends, receives, remote(
                    csnd.at[way, lay], chal.at[turn - 1, way, lay],
                    c_snd.at[turn - 1, way, lay], c_rcv.at[turn - 1, way, lay], to,
                )))
        return out

    g_copy = remote(dd.at[1], g_in, g_sem.at[0], g_sem.at[1], {"tm": 2})

    def chain(turn):
        for group, comp in ((0, 0), (0, 1), (1, 0), (1, 1), (2, 0), (2, 1)):
            for n, rows in d_pieces(group, comp):
                remote(
                    d_own.at[comp, rows], dd.at[turn - 1, comp, rows],
                    d_snd.at[0, n], d_rcv.at[turn - 1, n], {"tm": 0},
                ).wait_recv()

        taken = jnp.where(turn == 2, 1.0, 0.0)
        pl.when(turn == 2)(rs_copy.wait_recv)

        @pl.when(turn == 1)
        def _():
            for j in range(CROWS):
                mca[j + 1, middle, :] = dd[0, 0, j]
                sc[j] = dd[0, 1, j]

        @pl.when(turn > 1)
        def _():
            for j in range(CROWS):
                mca[j + 1, middle, :] = (dd[turn - 1, 0, j] - taken * rs_next[0, j]) + dd[turn - 2, 0, j]
                sc[j] = (dd[turn - 1, 1, j] - taken * rs_next[1, j]) + dd[turn - 2, 1, j]

        @pl.when(turn > 1)
        def _():
            for sends, _, copy in coarse_edge_copies(turn - 1):
                pl.when(sends)(copy.wait_send)

        for way, j, coef in ((0, CROWS - 1, pc1), (1, 0, nc1)):
            mid, out, _ = coarse_row(mca, j)
            mcb[j + 1, middle, :] = out
            factor = coef[j + 1]
            csnd[way, 0] = factor * mid
            csnd[way, 1] = factor * out
        for sends, _, copy in coarse_edge_copies(turn):
            pl.when(sends)(copy.start)

        for j in (0, CROWS - 1):
            old = sc[j]
            sc[j] = (old - bec[j] * old) + alc[j] * mca[j + 1, middle, :]
        for j in range(1, CROWS - 1):
            _, out, held = coarse_row(mca, j)
            mcb[j + 1, middle, :] = out
            sc[j] = held
        coarse_second(turn, *range(2, CROWS - 2))

        @pl.when(turn == 1)
        def _():
            pl.when(has_dn)(cst_up.wait_recv)
            pl.when(has_up)(cst_dn.wait_recv)

        for _, receives, copy in coarse_edge_copies(turn):
            pl.when(receives)(copy.wait_recv)
        mcb[1, middle, :] = mcb[1, middle, :] + chal[turn - 1, 0, 0]
        mcb[CROWS, middle, :] = mcb[CROWS, middle, :] + chal[turn - 1, 1, 0]
        mcb[0, middle, :] = chal[turn - 1, 0, 1] + cst[0] * csnd[1, 0]
        mcb[CROWS + 1, middle, :] = chal[turn - 1, 1, 1] + cst[1] * csnd[0, 0]
        coarse_second(turn, 0, CROWS - 1, 1, CROWS - 2)

        pl.when(turn == 2)(g_copy.start)

    @pl.when(runs)
    def _():
        turns = jnp.where(is_last, LAST, 1)
        each(turns, lambda n: chain(n + 1))

        def result(j):
            g_out[0, j] = dd[turns - 1, 0, j]
            g_out[1, j] = dd[turns - 1, 1, j]

        each(CROWS, result)
        pl.when(is_last)(g_copy.wait_send)
        for sends, _, copy in coarse_edge_copies(turns):
            pl.when(sends)(copy.wait_send)
        pl.when(has_up)(cst_up.wait_send)
        pl.when(has_dn)(cst_dn.wait_send)

    @pl.when(t == 2)
    def _():
        g_copy.wait_recv()

        def result(j):
            g_out[0, j] = g_in[0, j]
            g_out[1, j] = g_in[1, j]

        each(CROWS, result)

    @pl.when(t == 0)
    def _():
        def result(j):
            g_out[0, j] = jnp.zeros((HALF, HALF), F32)
            g_out[1, j] = jnp.zeros((HALF, HALF), F32)

        each(CROWS, result)
        for copy in d_copies(0, 1) + d_copies(0, 1, 2, to=1):
            copy.wait_send()

    @pl.when(jnp.logical_or(t == 1, t == 2))
    def _():
        for copy in d_copies(0, 1, 2):
            copy.wait_send()

    each(CHUNKS, lambda c: wait_edges(1, c))
    pl.when(has_up)(st_up.wait_send)
    pl.when(has_dn)(st_dn.wait_send)
    pl.when(has_dn)(fw[0].wait_send)
    pl.when(has_up)(fw[1].wait_send)
    pl.when(t > 0)(rs_copy.wait_send)


def final_kernel(ends, g, out, buf, sem):
    wide = (iota((HALF, SIDE), 0) == (iota((HALF, SIDE), 1) // 2)).astype(F32).astype(BF16)
    tall = ((iota((SIDE, HALF), 0) // 2) == iota((SIDE, HALF), 1)).astype(F32).astype(BF16)

    def copy(comp, i):
        return pltpu.make_async_copy(buf.at[comp, i], out.at[comp, i], sem.at[comp, i])

    def body(n):
        comp, j = n // CROWS, n % CROWS
        spread = None
        for part in split(g[comp, j]):
            term = dot(tall, dot(part, wide).astype(BF16))
            spread = term if spread is None else spread + term
        for b in range(2):
            buf[comp, 2 * j + b] = ends[comp, 2 * j + b] + spread
            copy(comp, 2 * j + b).start()

    each(2 * CROWS, body, unroll=2)
    each(2 * ROWS, lambda n: copy(n // ROWS, n % ROWS).wait())


def per_device(start_states, velocity, site_class, attach_rates, detach_rates):
    any_ref = pl.BlockSpec(memory_space=pl.ANY)
    smem = pl.BlockSpec(memory_space=pltpu.SMEM)
    vmem = pl.BlockSpec(memory_space=pltpu.VMEM)
    start = start_states.reshape(start_states.shape[1:])
    plane = (SIDE, SIDE)
    cplane = (HALF, HALF)
    coarse = (2, CROWS) + cplane

    def buf(*shape):
        return pltpu.VMEM(shape, F32)

    brick = buf(ROWS, *plane)
    cbrick = buf(CROWS, *cplane)
    dma = pltpu.SemaphoreType.DMA
    ends, g = pl.pallas_call(
        main_kernel,
        out_shape=(pltpu.VMEM((2, ROWS) + plane, F32), pltpu.VMEM(coarse, F32)),
        in_specs=[any_ref, any_ref, any_ref, smem, smem],
        out_specs=(vmem, vmem),
        scratch_shapes=[
            buf(ROWS + 2, SIDE + 2 * PAD, SIDE), buf(ROWS + 2, SIDE + 2 * PAD, SIDE),
            buf(ROWS + 2, *plane), buf(ROWS + 2, *plane), brick, brick, brick, brick, brick, brick, brick,
            pltpu.VMEM((8,) + plane, jnp.int32),
            buf(2, 2, *plane), buf(2, 2, 2, *plane), buf(2, *plane),
            buf(*coarse), buf(*coarse), buf(*coarse), buf(3, *coarse), buf(*coarse),
            buf(CROWS + 2, HALF + 2 * PAD, HALF), buf(CROWS + 2, HALF + 2 * PAD, HALF), cbrick,
            buf(CROWS + 2, *cplane), buf(CROWS + 2, *cplane), cbrick, cbrick, cbrick, cbrick, cbrick, cbrick, cbrick,
            buf(2, 2, *cplane), buf(3, 2, 2, *cplane), buf(2, *cplane), buf(PLANES, SIDE, HALF),
            dma((6, ROWS)), dma((2, 2, 2, CHUNKS)), dma((2, 2, 2, CHUNKS)), dma((2,)), dma((2,)), dma((2,)), dma((2,)),
            dma((2,)), pltpu.SemaphoreType.REGULAR, dma((2, 10)), dma((3, 10)), dma((2,)), dma((3, 2, 2)), dma((3, 2, 2)), dma((2,)), dma((2,)),
        ],
        compiler_params=pltpu.CompilerParams(
            collective_id=0, has_side_effects=True, vmem_limit_bytes=56 * 1024 * 1024
        ),
    )(start, velocity, site_class, attach_rates, detach_rates)
    out = pl.pallas_call(
        final_kernel,
        out_shape=jax.ShapeDtypeStruct((2, ROWS) + plane, F32),
        in_specs=[vmem, vmem],
        out_specs=any_ref,
        scratch_shapes=[buf(2, ROWS, *plane), dma((2, ROWS))],
        compiler_params=pltpu.CompilerParams(vmem_limit_bytes=40 * 1024 * 1024),
    )(ends, g)
    return out[None]


def solution(mesh):
    in_specs = (
        P("tm", None, "space", None, None),
        P(None, "space", None, None),
        P("space", None, None),
        P(),
        P(),
    )
    return jax.shard_map(
        per_device, mesh=mesh, in_specs=in_specs, out_specs=P("tm", None, "space", None, None), check_vma=False
    )
```

```python
import jax
import jax.numpy as jnp
from jax import lax
from jax.experimental import pallas as pl
from jax.experimental.pallas import tpu as pltpu
from jax.sharding import PartitionSpec as P

MESH = pl.DeviceIdType.MESH
F32 = jnp.float32
BF16 = jnp.bfloat16

ROWS = 12
SIDE = 256
HALF = SIDE // 2
CROWS = ROWS // 2
PAD = 8
CHUNKS = 8
WIDE = SIDE // CHUNKS
SUB = 32
COEF = 128
PLANES = 4
SPREAD = 0.08
LAST = 3


def iota(shape, axis):
    return lax.broadcasted_iota(jnp.int32, shape, axis)


def pair_columns(scale):
    match = (iota((SIDE, HALF), 0) // 2) == iota((SIDE, HALF), 1)
    return jnp.where(match, scale, 0.0).astype(BF16)


def split(values):
    high = values.astype(BF16)
    return high, (values - high.astype(F32)).astype(BF16)


def dot(left, right):
    return jnp.dot(left, right, preferred_element_type=F32)


def each(count, body, unroll=1):
    lax.fori_loop(0, count, lambda i, _: (body(i), 0)[1], 0, unroll=unroll)


def main_kernel(
    start, velocity, site_class, attach_table, detach_table,
    ends, g_out,
    ma, mb, p1, n1, p2, n2, p3, n3, cc, al, be, cls,
    snd, hal, st,
    rs_own, rs_next, d_own, dd, g_in,
    mca, mcb, sc, pc1, nc1, pc2, nc2, pc3, nc3, ccc, alc, bec,
    csnd, chal, cst, tmp,
    load_sem, snd_sem, hal_sem, st_snd, st_rcv, fw_snd, fw_rcv,
    rs_sem, turn_sem, d_snd, d_rcv, g_sem, c_snd, c_rcv, cst_snd, cst_rcv,
):
    t = lax.axis_index("tm")
    s = lax.axis_index("space")
    has_up = s < 31
    has_dn = s > 0
    up = {"space": jnp.minimum(s + 1, 31)}
    dn = {"space": jnp.maximum(s - 1, 0)}
    core = t % 2
    sibling = {"tm": t + 1 - 2 * core}

    def remote(src, dst, send, recv, to):
        return pltpu.make_async_remote_copy(
            src_ref=src, dst_ref=dst, send_sem=send, recv_sem=recv,
            device_id=to, device_id_type=MESH,
        )

    barrier = pltpu.get_barrier_semaphore()
    for j in (1, 2, 3):
        pl.semaphore_signal(barrier, inc=1, device_id={"tm": (t + j) % 4}, device_id_type=MESH)

    @pl.when(has_up)
    def _():
        pl.semaphore_signal(barrier, inc=1, device_id=up, device_id_type=MESH)

    @pl.when(has_dn)
    def _():
        pl.semaphore_signal(barrier, inc=1, device_id=dn, device_id_type=MESH)

    def loads(i):
        inner = pl.ds(PAD, SIDE)
        pairs = (
            (velocity.at[0, i], p1.at[i + 1]),
            (velocity.at[1, i], p2.at[i]),
            (velocity.at[2, i], p3.at[i]),
            (site_class.at[i], cls.at[slot(i)]),
            (start.at[0, i], ma.at[i + 1, inner]),
            (start.at[1, i], ends.at[1, i]),
        )
        return [pltpu.make_async_copy(a, b, load_sem.at[j, i]) for j, (a, b) in enumerate(pairs)]

    def slot(i):
        return jnp.where(i < CROWS, 2 * i, 2 * (ROWS - 1 - i) + 1) % 8

    def order(k):
        return jnp.where(k % 2 == 0, k // 2, ROWS - 1 - k // 2)

    def start_loads(k):
        for copy in loads(order(k)):
            copy.start()

    each(4, start_loads)

    blank = jnp.zeros((PAD, SIDE), F32)

    def clear(i):
        for ref in (ma, mb):
            ref[i, pl.ds(0, PAD), :] = blank
            ref[i, pl.ds(PAD + SIDE, PAD), :] = blank

    each(ROWS + 2, clear)

    def clear_rows(c):
        rows = pl.ds(PAD + c * SUB, SUB)
        plain = pl.ds(c * SUB, SUB)
        zero = jnp.zeros((SUB, SIDE), F32)
        one = jnp.ones((SUB, SIDE), F32)
        for ref in (ma, mb):
            ref[0, rows, :] = zero
            ref[ROWS + 1, rows, :] = zero
        p1[0, plain, :] = one
        n1[ROWS + 1, plain, :] = one

        @pl.when(jnp.logical_not(has_dn))
        def _():
            st[0, plain, :] = zero
            for k in range(2):
                for lay in range(2):
                    hal[k, 0, lay, plain, :] = zero

        @pl.when(jnp.logical_not(has_up))
        def _():
            st[1, plain, :] = zero
            for k in range(2):
                for lay in range(2):
                    hal[k, 1, lay, plain, :] = zero

    each(SIDE // SUB, clear_rows)

    columns_table = pair_columns(0.125)

    def restrict_pairs(items):
        for n, (read, _) in enumerate(items):
            high, low = split(read(0) + read(1))
            tmp[n] = dot(high, columns_table) + dot(low, columns_table)
        for n, (_, write) in enumerate(items):
            write(tmp[n, pl.ds(0, HALF, 2), :] + tmp[n, pl.ds(1, HALF, 2), :])

    def put(ref, *index):
        def write(value):
            ref[index] = value
        return write

    def restrict_shifted(*pairs):
        items = []
        for j in pairs:
            items.append((lambda b, j=j: p2[2 * j + b], put(pc2, j)))
            items.append((lambda b, j=j: p3[2 * j + b], put(pc3, j)))
        restrict_pairs(items)

    row8 = iota((COEF, SIDE), 0)
    lane = iota((COEF, SIDE), 1)

    def fine_coefs(i):
        def body(c, before):
            y = pl.multiple_of(c * COEF, COEF)
            rows = pl.ds(y, COEF)
            u1 = p1[i + 1, rows, :]
            u2 = p2[i, rows, :]
            u3 = p3[i, rows, :]
            after = p2[i, pl.ds(pl.multiple_of(jnp.minimum(y + COEF, SIDE - PAD), PAD), PAD), :]
            wide = jnp.concatenate([before, u2, after], axis=0)
            wide_plus = jnp.maximum(wide, 0.0) + SPREAD
            wide_minus = wide_plus - wide
            plus1 = jnp.maximum(u1, 0.0) + SPREAD
            minus1 = plus1 - u1
            plus3 = jnp.maximum(u3, 0.0) + SPREAD
            minus3 = plus3 - u3
            kind = cls[slot(i), rows, :]
            attach = jnp.zeros((COEF, SIDE), F32)
            detach = jnp.zeros((COEF, SIDE), F32)
            for level in range(8):
                here = kind == level
                attach = jnp.where(here, attach_table[level], attach)
                detach = jnp.where(here, detach_table[level], detach)
            total = plus1 + minus1 + wide_plus[PAD:PAD + COEF] + wide_minus[PAD:PAD + COEF] + plus3 + minus3
            p1[i + 1, rows, :] = plus1
            n1[i + 1, rows, :] = minus1
            p2[i, rows, :] = jnp.where(row8 + y == 0, 0.0, wide_plus[PAD - 1:PAD - 1 + COEF])
            n2[i, rows, :] = jnp.where(row8 + y == SIDE - 1, 0.0, wide_minus[PAD + 1:PAD + 1 + COEF])
            p3[i, rows, :] = jnp.where(lane == 0, 0.0, pltpu.roll(plus3, 1, 1))
            n3[i, rows, :] = jnp.where(lane == SIDE - 1, 0.0, pltpu.roll(minus3, SIDE - 1, 1))
            cc[i, rows, :] = (1.0 - total) - attach
            al[i, rows, :] = attach
            be[i, rows, :] = detach
            return u2[COEF - PAD:]

        lax.fori_loop(0, SIDE // COEF, body, jnp.zeros((PAD, SIDE), F32), unroll=SIDE // COEF)

    sv = ends.at[1]

    def fine_row(src, i, y, size):
        rows = pl.ds(y, size)
        wide = src[i + 1, pl.ds(y, size + 2 * PAD), :]
        mid = wide[PAD:PAD + size]
        old = sv[i, rows, :]
        off = be[i, rows, :] * old
        padded = pl.ds(y + PAD, size)
        out = cc[i, rows, :] * mid + off
        out = out + (p1[i, rows, :] * src[i, padded, :] + n1[i + 2, rows, :] * src[i + 2, padded, :])
        out = out + (p2[i, rows, :] * wide[PAD - 1:PAD - 1 + size] + n2[i, rows, :] * wide[PAD + 1:PAD + 1 + size])
        out = out + (p3[i, rows, :] * pltpu.roll(mid, 1, 1) + n3[i, rows, :] * pltpu.roll(mid, SIDE - 1, 1))
        return mid, out, (old - off) + al[i, rows, :] * mid

    def step_row(src, write, i, y, size):
        _, out, held = fine_row(src, i, y, size)
        write(i, y, size, out)
        sv[i, pl.ds(y, size), :] = held

    def write_a(i, y, size, out):
        ma[i + 1, pl.ds(y + PAD, size), :] = out

    def write_b(i, y, size, out):
        mb[i + 1, pl.ds(y + PAD, size), :] = out

    def write_end(i, y, size, out):
        ends[0, i, pl.ds(y, size), :] = out

    def attach_edge(i):
        old = sv[i]
        sv[i] = (old - be[i] * old) + al[i] * ma[i + 1, pl.ds(PAD, SIDE), :]

    def edge_copies(k, c):
        rows = pl.ds(c * WIDE, WIDE)
        out = []
        for way, (to, sends, receives) in enumerate(((up, has_up, has_dn), (dn, has_dn, has_up))):
            for lay in range(2):
                out.append((sends, receives, remote(
                    snd.at[way, lay, rows], hal.at[k, way, lay, rows],
                    snd_sem.at[k, way, lay, c], hal_sem.at[k, way, lay, c], to,
                )))
        return out

    def send_edges(k, c):
        y = pl.multiple_of(c * WIDE, WIDE)
        rows = pl.ds(y, WIDE)
        for way, i, coef in ((0, ROWS - 1, p1), (1, 0, n1)):
            mid, out, _ = fine_row(ma, i, y, WIDE)
            mb[i + 1, pl.ds(y + PAD, WIDE), :] = out
            factor = coef[i + 1, rows, :]
            snd[way, 0, rows, :] = factor * mid
            snd[way, 1, rows, :] = factor * out
        for sends, _, copy in edge_copies(k, c):
            pl.when(sends)(copy.start)

    def take_edges(k, c):
        for _, receives, copy in edge_copies(k, c):
            pl.when(receives)(copy.wait_recv)

        y = pl.multiple_of(c * WIDE, WIDE)
        rows = pl.ds(y, WIDE)
        padded = pl.ds(y + PAD, WIDE)
        mb[1, padded, :] = mb[1, padded, :] + hal[k, 0, 0, rows, :]
        mb[ROWS, padded, :] = mb[ROWS, padded, :] + hal[k, 1, 0, rows, :]
        mb[0, padded, :] = hal[k, 0, 1, rows, :] + st[0, rows, :] * snd[1, 0, rows, :]
        mb[ROWS + 1, padded, :] = hal[k, 1, 1, rows, :] + st[1, rows, :] * snd[0, 0, rows, :]

    def edge_step(write, c):
        y = pl.multiple_of(c * WIDE, WIDE)
        for i in (0, ROWS - 1, 1, ROWS - 2):
            step_row(mb, write, i, y, WIDE)

    def wait_edges(k, c):
        for sends, _, copy in edge_copies(k, c):
            pl.when(sends)(copy.wait_send)

    def start_kinds(k):
        i = order(k + 8)
        pltpu.make_async_copy(site_class.at[i], cls.at[slot(i)], load_sem.at[3, i]).start()

    def ready(k):
        for copy in loads(order(k)):
            copy.wait()
        start_loads(k + 4)
        for n, copy in enumerate(loads(order(k + 8))):
            if n != 3:
                copy.start()

    each(4, ready)
    restrict_shifted(0, CROWS - 1)
    each(4, lambda k: fine_coefs(order(k)))
    each(4, start_kinds)

    pl.semaphore_wait(barrier, 3 + has_up.astype(jnp.int32) + has_dn.astype(jnp.int32))

    own_half = pl.ds(core * HALF, HALF)
    other_half = pl.ds((1 - core) * HALF, HALF)
    st_up = remote(p1.at[ROWS, own_half], st.at[0, own_half], st_snd.at[0], st_rcv.at[0], up)
    st_dn = remote(n1.at[1, own_half], st.at[1, own_half], st_snd.at[1], st_rcv.at[1], dn)
    pl.when(has_up)(st_up.start)
    pl.when(has_dn)(st_dn.start)

    each(CHUNKS, lambda c: send_edges(0, c))

    def more_coefs(p):
        def row(n):
            return jnp.where(n < 2, 2 * p, 2 * (CROWS - 1 - p) - 2) + n

        def arrived(n):
            for copy in loads(row(n))[:4]:
                copy.wait()

        each(4, arrived)
        restrict_shifted(p, CROWS - 1 - p)
        each(4, lambda n: fine_coefs(row(n)))

    def state_arrived(k):
        for copy in loads(order(k + 4))[4:]:
            copy.wait()

    each(ROWS - 4, state_arrived)

    inner = pl.ds(PAD, SIDE)

    def restrict_start(n):
        items = []
        for j in (2 * n, 2 * n + 1):
            items.append((lambda b, j=j: ma[2 * j + b + 1, inner, :], put(rs_own, 0, j)))
            items.append((lambda b, j=j: sv[2 * j + b], put(rs_own, 1, j)))
        restrict_pairs(items)

    each(CROWS // 2, restrict_start)

    rs_copy = remote(rs_own, rs_next, rs_sem.at[0], rs_sem.at[1], sibling)
    @pl.when(t == 1)
    def _():
        for comp in range(2):
            for j in range(CROWS):
                rs_next[comp, j] = jnp.zeros((HALF, HALF), F32)

    pl.when(t > 0)(rs_copy.start)

    fw = [remote(st.at[w, own_half], st.at[w, own_half], fw_snd.at[w], fw_rcv.at[w], sibling) for w in range(2)]
    fr = [remote(st.at[w, other_half], st.at[w, other_half], fw_snd.at[w], fw_rcv.at[w], sibling) for w in range(2)]
    def share_static():
        for w, exists, copy in ((0, has_dn, st_up), (1, has_up, st_dn)):
            @pl.when(exists)
            def _(w=w, copy=copy):
                copy.wait_recv()
                fw[w].start()
        for w, exists in ((0, has_dn), (1, has_up)):
            pl.when(exists)(fr[w].wait_recv)

    def restrict_static(j):
        restrict_pairs((
            (lambda b: p1[2 * j + b + 1] - n1[2 * j + b + 1], put(pc1, j + 1)),
            (lambda b: 2.0 * al[2 * j + b], put(alc, j)),
            (lambda b: 2.0 * be[2 * j + b], put(bec, j)),
        ))

    crow = iota((HALF, HALF), 0)
    clane = iota((HALF, HALF), 1)
    coarse_spread = 0.5 * SPREAD

    def coarse_coefs(j):
        u1, u2, u3 = pc1[j + 1], pc2[j], pc3[j]
        plus1 = jnp.maximum(u1, 0.0) + coarse_spread
        minus1 = plus1 - u1
        plus2 = jnp.maximum(u2, 0.0) + coarse_spread
        minus2 = plus2 - u2
        plus3 = jnp.maximum(u3, 0.0) + coarse_spread
        minus3 = plus3 - u3
        ccc[j] = (1.0 - (plus1 + minus1 + plus2 + minus2 + plus3 + minus3)) - alc[j]
        pc1[j + 1] = plus1
        nc1[j + 1] = minus1
        pc2[j] = jnp.where(crow == 0, 0.0, pltpu.roll(plus2, 1, 0))
        nc2[j] = jnp.where(crow == HALF - 1, 0.0, pltpu.roll(minus2, HALF - 1, 0))
        pc3[j] = jnp.where(clane == 0, 0.0, pltpu.roll(plus3, 1, 1))
        nc3[j] = jnp.where(clane == HALF - 1, 0.0, pltpu.roll(minus3, HALF - 1, 1))

    is_last = t == LAST
    runs = t % 2 == 1
    cst_up = remote(pc1.at[CROWS], cst.at[0], cst_snd.at[0], cst_rcv.at[0], up)
    cst_dn = remote(nc1.at[1], cst.at[1], cst_snd.at[1], cst_rcv.at[1], dn)

    def d_pieces(group, comp):
        if group == 0:
            return ((comp, pl.ds(2, 2)),)
        first = 2 - group
        return ((4 * group - 2 + comp, pl.ds(first, 1)), (4 * group + comp, pl.ds(CROWS - 1 - first, 1)))

    def d_copies(*groups, to=LAST):
        return [
            remote(
                d_own.at[comp, rows], dd.at[t, comp, rows],
                d_snd.at[0 if to == LAST else 1, n], d_rcv.at[t, n], {"tm": to},
            )
            for group in groups for comp in range(2) for n, rows in d_pieces(group, comp)
        ]

    def send_jump(*groups):
        for copy in d_copies(*groups):
            copy.start()

        @pl.when(t == 0)
        def _():
            for copy in d_copies(*groups, to=1):
                copy.start()

    keep = jnp.where(t == 1, 0.0, 1.0)

    def jump(*rows):
        def item(comp, j):
            def write(value):
                d_own[comp, j] = value - keep * rs_next[comp, j]
            return lambda b: ends[comp, 2 * j + b], write

        restrict_pairs([item(comp, j) for j in rows for comp in range(2)])

    def among(n, *values):
        found = n == values[0]
        for value in values[1:]:
            found = jnp.logical_or(found, n == value)
        return found

    def fill(n):
        outer = among(n, 1, 11)
        pl.when(among(n, 0, 2))(lambda: more_coefs(jnp.where(n == 0, 1, 2)))
        pl.when(outer)(lambda: (attach_edge(0), attach_edge(ROWS - 1), None)[2])

        @pl.when(among(n, 1, 3, 6, 11))
        def _():
            def body(m):
                first = jnp.where(outer, 1 + (ROWS - 4) * m, 3 + 2 * m)
                for b in range(2):
                    step_row(ma, write_b, first + b, 0, SIDE)

            each(jnp.where(outer, 2, 3), body)

        @pl.when(among(n, 4, 5))
        def _():
            each(4, lambda m: step_row(mb, write_a, 4 * n - 14 + m, 0, SIDE), unroll=2)

        @pl.when(among(n, 7, 11))
        def _():
            def body(m):
                first = jnp.where(outer, 2 + (ROWS - 6) * m, 4 + 2 * m)
                for b in range(2):
                    step_row(mb, write_end, first + b, 0, SIDE)

            each(2, body)

        @pl.when(jnp.logical_and(runs, jnp.logical_and(n >= 4, n < 10)))
        def _():
            restrict_static(n - 4)
            coarse_coefs(n - 4)

        @pl.when(jnp.logical_and(jnp.logical_not(is_last), among(n, 8, 11)))
        def _():
            pl.when(jnp.logical_and(n == 8, t != 1))(rs_copy.wait_recv)
            p = jnp.where(n == 8, 2, 1)
            jump(p, CROWS - 1 - p)
            pl.when(jnp.logical_and(n == 8, t != 1))(lambda: send_jump(0))
            pl.when(jnp.logical_and(n == 11, t != 1))(lambda: send_jump(1))

    def between(n):
        fill(n)
        pl.when(n == 1)(share_static)
        pl.when(jnp.logical_and(n >= 1, n <= CHUNKS))(lambda: take_edges(0, n - 1))
        pl.when(jnp.logical_and(n >= 2, n <= CHUNKS + 1))(lambda: edge_step(write_a, n - 2))

        @pl.when(jnp.logical_and(n >= 3, n <= CHUNKS + 2))
        def _():
            wait_edges(0, n - 3)
            send_edges(1, n - 3)

    each(CHUNKS + 4, between)

    @pl.when(runs)
    def _():
        pl.when(has_up)(cst_up.start)
        pl.when(has_dn)(cst_dn.start)
        zero = jnp.zeros((HALF, HALF), F32)
        one = jnp.ones((HALF, HALF), F32)
        pc1[0] = one
        nc1[CROWS + 1] = one
        margin = jnp.zeros((PAD, HALF), F32)
        middle = pl.ds(PAD, HALF)

        def margins(j):
            for ref in (mca, mcb):
                ref[j, pl.ds(0, PAD), :] = margin
                ref[j, pl.ds(PAD + HALF, PAD), :] = margin

        each(CROWS + 2, margins)
        for j in (0, CROWS + 1):
            mca[j, middle, :] = zero

        @pl.when(jnp.logical_not(has_dn))
        def _():
            cst[0] = zero
            for k in range(3):
                for lay in range(2):
                    chal[k, 0, lay] = zero

        @pl.when(jnp.logical_not(has_up))
        def _():
            cst[1] = zero
            for k in range(3):
                for lay in range(2):
                    chal[k, 1, lay] = zero

    def finish(n):
        pl.when(n < CHUNKS)(lambda: take_edges(1, n))
        pl.when(n >= 1)(lambda: edge_step(write_end, n - 1))

    each(CHUNKS + 1, finish)

    @pl.when(jnp.logical_not(is_last))
    def _():
        jump(0, CROWS - 1)

        @pl.when(t == 1)
        def _():
            pl.semaphore_wait(turn_sem, 1)
            for copy in d_copies(0, 1):
                copy.start()

        send_jump(2)

        @pl.when(t == 0)
        def _():
            first, second, *rest = d_copies(2)
            first.wait_send()
            second.wait_send()
            pl.semaphore_signal(turn_sem, inc=1, device_id={"tm": 1}, device_id_type=MESH)
            for copy in rest:
                copy.wait_send()

    middle = pl.ds(PAD, HALF)

    def coarse_row(src, j):
        wide = src[j + 1]
        mid = wide[PAD:PAD + HALF]
        old = sc[j]
        off = bec[j] * old
        out = ccc[j] * mid + off
        out = out + (pc1[j] * src[j, middle, :] + nc1[j + 2] * src[j + 2, middle, :])
        out = out + (pc2[j] * wide[PAD - 1:PAD - 1 + HALF] + nc2[j] * wide[PAD + 1:PAD + 1 + HALF])
        out = out + (pc3[j] * pltpu.roll(mid, 1, 1) + nc3[j] * pltpu.roll(mid, HALF - 1, 1))
        return mid, out, (old - off) + alc[j] * mid

    def coarse_second(turn, *rows):
        for j in rows:
            _, out, held = coarse_row(mcb, j)
            dd[turn - 1, 0, j] = out
            dd[turn - 1, 1, j] = held

    def coarse_edge_copies(turn):
        out = []
        for way, (to, sends, receives) in enumerate(((up, has_up, has_dn), (dn, has_dn, has_up))):
            for lay in range(2):
                out.append((sends, receives, remote(
                    csnd.at[way, lay], chal.at[turn - 1, way, lay],
                    c_snd.at[turn - 1, way, lay], c_rcv.at[turn - 1, way, lay], to,
                )))
        return out

    g_copy = remote(dd.at[1], g_in, g_sem.at[0], g_sem.at[1], {"tm": 2})

    def chain(turn):
        for group, comp in ((0, 0), (0, 1), (1, 0), (1, 1), (2, 0), (2, 1)):
            for n, rows in d_pieces(group, comp):
                remote(
                    d_own.at[comp, rows], dd.at[turn - 1, comp, rows],
                    d_snd.at[0, n], d_rcv.at[turn - 1, n], {"tm": 0},
                ).wait_recv()

        taken = jnp.where(turn == 2, 1.0, 0.0)
        pl.when(turn == 2)(rs_copy.wait_recv)

        @pl.when(turn == 1)
        def _():
            for j in range(CROWS):
                mca[j + 1, middle, :] = dd[0, 0, j]
                sc[j] = dd[0, 1, j]

        @pl.when(turn > 1)
        def _():
            for j in range(CROWS):
                mca[j + 1, middle, :] = (dd[turn - 1, 0, j] - taken * rs_next[0, j]) + dd[turn - 2, 0, j]
                sc[j] = (dd[turn - 1, 1, j] - taken * rs_next[1, j]) + dd[turn - 2, 1, j]

        @pl.when(turn > 1)
        def _():
            for sends, _, copy in coarse_edge_copies(turn - 1):
                pl.when(sends)(copy.wait_send)

        for way, j, coef in ((0, CROWS - 1, pc1), (1, 0, nc1)):
            mid, out, _ = coarse_row(mca, j)
            mcb[j + 1, middle, :] = out
            factor = coef[j + 1]
            csnd[way, 0] = factor * mid
            csnd[way, 1] = factor * out
        for sends, _, copy in coarse_edge_copies(turn):
            pl.when(sends)(copy.start)

        for j in (0, CROWS - 1):
            old = sc[j]
            sc[j] = (old - bec[j] * old) + alc[j] * mca[j + 1, middle, :]
        for j in range(1, CROWS - 1):
            _, out, held = coarse_row(mca, j)
            mcb[j + 1, middle, :] = out
            sc[j] = held
        coarse_second(turn, *range(2, CROWS - 2))

        @pl.when(turn == 1)
        def _():
            pl.when(has_dn)(cst_up.wait_recv)
            pl.when(has_up)(cst_dn.wait_recv)

        for _, receives, copy in coarse_edge_copies(turn):
            pl.when(receives)(copy.wait_recv)
        mcb[1, middle, :] = mcb[1, middle, :] + chal[turn - 1, 0, 0]
        mcb[CROWS, middle, :] = mcb[CROWS, middle, :] + chal[turn - 1, 1, 0]
        mcb[0, middle, :] = chal[turn - 1, 0, 1] + cst[0] * csnd[1, 0]
        mcb[CROWS + 1, middle, :] = chal[turn - 1, 1, 1] + cst[1] * csnd[0, 0]
        coarse_second(turn, 0, CROWS - 1, 1, CROWS - 2)

        pl.when(turn == 2)(g_copy.start)

    @pl.when(runs)
    def _():
        turns = jnp.where(is_last, LAST, 1)
        each(turns, lambda n: chain(n + 1))

        def result(j):
            g_out[0, j] = dd[turns - 1, 0, j]
            g_out[1, j] = dd[turns - 1, 1, j]

        each(CROWS, result)
        pl.when(is_last)(g_copy.wait_send)
        for sends, _, copy in coarse_edge_copies(turns):
            pl.when(sends)(copy.wait_send)
        pl.when(has_up)(cst_up.wait_send)
        pl.when(has_dn)(cst_dn.wait_send)

    @pl.when(t == 2)
    def _():
        g_copy.wait_recv()

        def result(j):
            g_out[0, j] = g_in[0, j]
            g_out[1, j] = g_in[1, j]

        each(CROWS, result)

    @pl.when(t == 0)
    def _():
        def result(j):
            g_out[0, j] = jnp.zeros((HALF, HALF), F32)
            g_out[1, j] = jnp.zeros((HALF, HALF), F32)

        each(CROWS, result)
        for copy in d_copies(0, 1) + d_copies(0, 1, 2, to=1):
            copy.wait_send()

    @pl.when(jnp.logical_or(t == 1, t == 2))
    def _():
        for copy in d_copies(0, 1, 2):
            copy.wait_send()

    each(CHUNKS, lambda c: wait_edges(1, c))
    pl.when(has_up)(st_up.wait_send)
    pl.when(has_dn)(st_dn.wait_send)
    pl.when(has_dn)(fw[0].wait_send)
    pl.when(has_up)(fw[1].wait_send)
    pl.when(t > 0)(rs_copy.wait_send)


def final_kernel(ends, g, out, buf, sem):
    wide = (iota((HALF, SIDE), 0) == (iota((HALF, SIDE), 1) // 2)).astype(F32).astype(BF16)
    tall = ((iota((SIDE, HALF), 0) // 2) == iota((SIDE, HALF), 1)).astype(F32).astype(BF16)

    def copy(comp, i):
        return pltpu.make_async_copy(buf.at[comp, i], out.at[comp, i], sem.at[comp, i])

    def body(n):
        comp, j = n // CROWS, n % CROWS
        spread = None
        for part in split(g[comp, j]):
            term = dot(tall, dot(part, wide).astype(BF16))
            spread = term if spread is None else spread + term
        for b in range(2):
            buf[comp, 2 * j + b] = ends[comp, 2 * j + b] + spread
            copy(comp, 2 * j + b).start()

    each(2 * CROWS, body, unroll=4)
    each(2 * ROWS, lambda n: copy(n // ROWS, n % ROWS).wait())


def per_device(start_states, velocity, site_class, attach_rates, detach_rates):
    any_ref = pl.BlockSpec(memory_space=pl.ANY)
    smem = pl.BlockSpec(memory_space=pltpu.SMEM)
    vmem = pl.BlockSpec(memory_space=pltpu.VMEM)
    start = start_states.reshape(start_states.shape[1:])
    plane = (SIDE, SIDE)
    cplane = (HALF, HALF)
    coarse = (2, CROWS) + cplane

    def buf(*shape):
        return pltpu.VMEM(shape, F32)

    brick = buf(ROWS, *plane)
    cbrick = buf(CROWS, *cplane)
    dma = pltpu.SemaphoreType.DMA
    ends, g = pl.pallas_call(
        main_kernel,
        out_shape=(pltpu.VMEM((2, ROWS) + plane, F32), pltpu.VMEM(coarse, F32)),
        in_specs=[any_ref, any_ref, any_ref, smem, smem],
        out_specs=(vmem, vmem),
        scratch_shapes=[
            buf(ROWS + 2, SIDE + 2 * PAD, SIDE), buf(ROWS + 2, SIDE + 2 * PAD, SIDE),
            buf(ROWS + 2, *plane), buf(ROWS + 2, *plane), brick, brick, brick, brick, brick, brick, brick,
            pltpu.VMEM((8,) + plane, jnp.int32),
            buf(2, 2, *plane), buf(2, 2, 2, *plane), buf(2, *plane),
            buf(*coarse), buf(*coarse), buf(*coarse), buf(3, *coarse), buf(*coarse),
            buf(CROWS + 2, HALF + 2 * PAD, HALF), buf(CROWS + 2, HALF + 2 * PAD, HALF), cbrick,
            buf(CROWS + 2, *cplane), buf(CROWS + 2, *cplane), cbrick, cbrick, cbrick, cbrick, cbrick, cbrick, cbrick,
            buf(2, 2, *cplane), buf(3, 2, 2, *cplane), buf(2, *cplane), buf(PLANES, SIDE, HALF),
            dma((6, ROWS)), dma((2, 2, 2, CHUNKS)), dma((2, 2, 2, CHUNKS)), dma((2,)), dma((2,)), dma((2,)), dma((2,)),
            dma((2,)), pltpu.SemaphoreType.REGULAR, dma((2, 10)), dma((3, 10)), dma((2,)), dma((3, 2, 2)), dma((3, 2, 2)), dma((2,)), dma((2,)),
        ],
        compiler_params=pltpu.CompilerParams(
            collective_id=0, has_side_effects=True, vmem_limit_bytes=56 * 1024 * 1024
        ),
    )(start, velocity, site_class, attach_rates, detach_rates)
    out = pl.pallas_call(
        final_kernel,
        out_shape=jax.ShapeDtypeStruct((2, ROWS) + plane, F32),
        in_specs=[vmem, vmem],
        out_specs=any_ref,
        scratch_shapes=[buf(2, ROWS, *plane), dma((2, ROWS))],
        compiler_params=pltpu.CompilerParams(vmem_limit_bytes=40 * 1024 * 1024),
    )(ends, g)
    return out[None]


def solution(mesh):
    in_specs = (
        P("tm", None, "space", None, None),
        P(None, "space", None, None),
        P("space", None, None),
        P(),
        P(),
    )
    return jax.shard_map(
        per_device, mesh=mesh, in_specs=in_specs, out_specs=P("tm", None, "space", None, None), check_vma=False
    )
```

```python
import jax
import jax.numpy as jnp
from jax import lax
from jax.experimental import pallas as pl
from jax.experimental.pallas import tpu as pltpu
from jax.sharding import PartitionSpec as P

MESH = pl.DeviceIdType.MESH
F32 = jnp.float32
BF16 = jnp.bfloat16

ROWS = 12
SIDE = 256
HALF = SIDE // 2
CROWS = ROWS // 2
PAD = 8
CHUNKS = 8
WIDE = SIDE // CHUNKS
SUB = 32
COEF = 128
PLANES = 4
SPREAD = 0.08
LAST = 3


def iota(shape, axis):
    return lax.broadcasted_iota(jnp.int32, shape, axis)


def pair_columns(scale):
    match = (iota((SIDE, HALF), 0) // 2) == iota((SIDE, HALF), 1)
    return jnp.where(match, scale, 0.0).astype(BF16)


def split(values):
    high = values.astype(BF16)
    return high, (values - high.astype(F32)).astype(BF16)


def dot(left, right):
    return jnp.dot(left, right, preferred_element_type=F32)


def each(count, body, unroll=1):
    lax.fori_loop(0, count, lambda i, _: (body(i), 0)[1], 0, unroll=unroll)


def main_kernel(
    start, velocity, site_class, attach_table, detach_table,
    ends, g_out,
    ma, mb, p1, n1, p2, n2, p3, n3, cc, al, be, cls,
    snd, hal, st,
    rs_own, rs_next, d_own, dd, g_in,
    mca, mcb, sc, pc1, nc1, pc2, nc2, pc3, nc3, ccc, alc, bec,
    csnd, chal, cst, tmp,
    load_sem, snd_sem, hal_sem, st_snd, st_rcv, fw_snd, fw_rcv,
    rs_sem, turn_sem, d_snd, d_rcv, g_sem, c_snd, c_rcv, cst_snd, cst_rcv,
):
    t = lax.axis_index("tm")
    s = lax.axis_index("space")
    has_up = s < 31
    has_dn = s > 0
    up = {"space": jnp.minimum(s + 1, 31)}
    dn = {"space": jnp.maximum(s - 1, 0)}
    core = t % 2
    sibling = {"tm": t + 1 - 2 * core}

    def remote(src, dst, send, recv, to):
        return pltpu.make_async_remote_copy(
            src_ref=src, dst_ref=dst, send_sem=send, recv_sem=recv,
            device_id=to, device_id_type=MESH,
        )

    barrier = pltpu.get_barrier_semaphore()
    for j in (1, 2, 3):
        pl.semaphore_signal(barrier, inc=1, device_id={"tm": (t + j) % 4}, device_id_type=MESH)

    @pl.when(has_up)
    def _():
        pl.semaphore_signal(barrier, inc=1, device_id=up, device_id_type=MESH)

    @pl.when(has_dn)
    def _():
        pl.semaphore_signal(barrier, inc=1, device_id=dn, device_id_type=MESH)

    def loads(i):
        inner = pl.ds(PAD, SIDE)
        pairs = (
            (velocity.at[0, i], p1.at[i + 1]),
            (velocity.at[1, i], p2.at[i]),
            (velocity.at[2, i], p3.at[i]),
            (site_class.at[i], cls.at[slot(i)]),
            (start.at[0, i], ma.at[i + 1, inner]),
            (start.at[1, i], ends.at[1, i]),
        )
        return [pltpu.make_async_copy(a, b, load_sem.at[j, i]) for j, (a, b) in enumerate(pairs)]

    def slot(i):
        return jnp.where(i < CROWS, 2 * i, 2 * (ROWS - 1 - i) + 1) % 8

    def order(k):
        return jnp.where(k % 2 == 0, k // 2, ROWS - 1 - k // 2)

    def start_loads(k):
        for copy in loads(order(k)):
            copy.start()

    each(4, start_loads)

    blank = jnp.zeros((PAD, SIDE), F32)

    def clear(i):
        for ref in (ma, mb):
            ref[i, pl.ds(0, PAD), :] = blank
            ref[i, pl.ds(PAD + SIDE, PAD), :] = blank

    each(ROWS + 2, clear)

    def clear_rows(c):
        rows = pl.ds(PAD + c * SUB, SUB)
        plain = pl.ds(c * SUB, SUB)
        zero = jnp.zeros((SUB, SIDE), F32)
        one = jnp.ones((SUB, SIDE), F32)
        for ref in (ma, mb):
            ref[0, rows, :] = zero
            ref[ROWS + 1, rows, :] = zero
        p1[0, plain, :] = one
        n1[ROWS + 1, plain, :] = one

        @pl.when(jnp.logical_not(has_dn))
        def _():
            st[0, plain, :] = zero
            for k in range(2):
                for lay in range(2):
                    hal[k, 0, lay, plain, :] = zero

        @pl.when(jnp.logical_not(has_up))
        def _():
            st[1, plain, :] = zero
            for k in range(2):
                for lay in range(2):
                    hal[k, 1, lay, plain, :] = zero

    each(SIDE // SUB, clear_rows)

    columns_table = pair_columns(0.125)

    def restrict_pairs(items):
        for n, (read, _) in enumerate(items):
            high, low = split(read(0) + read(1))
            tmp[n] = dot(high, columns_table) + dot(low, columns_table)
        for n, (_, write) in enumerate(items):
            write(tmp[n, pl.ds(0, HALF, 2), :] + tmp[n, pl.ds(1, HALF, 2), :])

    def put(ref, *index):
        def write(value):
            ref[index] = value
        return write

    def restrict_shifted(*pairs):
        items = []
        for j in pairs:
            items.append((lambda b, j=j: p2[2 * j + b], put(pc2, j)))
            items.append((lambda b, j=j: p3[2 * j + b], put(pc3, j)))
        restrict_pairs(items)

    row8 = iota((COEF, SIDE), 0)
    lane = iota((COEF, SIDE), 1)

    def fine_coefs(i):
        def body(c, before):
            y = pl.multiple_of(c * COEF, COEF)
            rows = pl.ds(y, COEF)
            u1 = p1[i + 1, rows, :]
            u2 = p2[i, rows, :]
            u3 = p3[i, rows, :]
            after = p2[i, pl.ds(pl.multiple_of(jnp.minimum(y + COEF, SIDE - PAD), PAD), PAD), :]
            wide = jnp.concatenate([before, u2, after], axis=0)
            wide_plus = jnp.maximum(wide, 0.0) + SPREAD
            wide_minus = wide_plus - wide
            plus1 = jnp.maximum(u1, 0.0) + SPREAD
            minus1 = plus1 - u1
            plus3 = jnp.maximum(u3, 0.0) + SPREAD
            minus3 = plus3 - u3
            kind = cls[slot(i), rows, :]
            attach = jnp.zeros((COEF, SIDE), F32)
            detach = jnp.zeros((COEF, SIDE), F32)
            for level in range(8):
                here = kind == level
                attach = jnp.where(here, attach_table[level], attach)
                detach = jnp.where(here, detach_table[level], detach)
            total = plus1 + minus1 + wide_plus[PAD:PAD + COEF] + wide_minus[PAD:PAD + COEF] + plus3 + minus3
            p1[i + 1, rows, :] = plus1
            n1[i + 1, rows, :] = minus1
            p2[i, rows, :] = jnp.where(row8 + y == 0, 0.0, wide_plus[PAD - 1:PAD - 1 + COEF])
            n2[i, rows, :] = jnp.where(row8 + y == SIDE - 1, 0.0, wide_minus[PAD + 1:PAD + 1 + COEF])
            p3[i, rows, :] = jnp.where(lane == 0, 0.0, pltpu.roll(plus3, 1, 1))
            n3[i, rows, :] = jnp.where(lane == SIDE - 1, 0.0, pltpu.roll(minus3, SIDE - 1, 1))
            cc[i, rows, :] = (1.0 - total) - attach
            al[i, rows, :] = attach
            be[i, rows, :] = detach
            return u2[COEF - PAD:]

        lax.fori_loop(0, SIDE // COEF, body, jnp.zeros((PAD, SIDE), F32), unroll=SIDE // COEF)

    sv = ends.at[1]

    def fine_row(src, i, y, size):
        rows = pl.ds(y, size)
        wide = src[i + 1, pl.ds(y, size + 2 * PAD), :]
        mid = wide[PAD:PAD + size]
        old = sv[i, rows, :]
        off = be[i, rows, :] * old
        padded = pl.ds(y + PAD, size)
        out = cc[i, rows, :] * mid + off
        out = out + (p1[i, rows, :] * src[i, padded, :] + n1[i + 2, rows, :] * src[i + 2, padded, :])
        out = out + (p2[i, rows, :] * wide[PAD - 1:PAD - 1 + size] + n2[i, rows, :] * wide[PAD + 1:PAD + 1 + size])
        out = out + (p3[i, rows, :] * pltpu.roll(mid, 1, 1) + n3[i, rows, :] * pltpu.roll(mid, SIDE - 1, 1))
        return mid, out, (old - off) + al[i, rows, :] * mid

    def step_row(src, write, i, y, size):
        _, out, held = fine_row(src, i, y, size)
        write(i, y, size, out)
        sv[i, pl.ds(y, size), :] = held

    def write_a(i, y, size, out):
        ma[i + 1, pl.ds(y + PAD, size), :] = out

    def write_b(i, y, size, out):
        mb[i + 1, pl.ds(y + PAD, size), :] = out

    def write_end(i, y, size, out):
        ends[0, i, pl.ds(y, size), :] = out

    def attach_edge(i):
        old = sv[i]
        sv[i] = (old - be[i] * old) + al[i] * ma[i + 1, pl.ds(PAD, SIDE), :]

    def edge_copies(k, c):
        rows = pl.ds(c * WIDE, WIDE)
        out = []
        for way, (to, sends, receives) in enumerate(((up, has_up, has_dn), (dn, has_dn, has_up))):
            for lay in range(2):
                out.append((sends, receives, remote(
                    snd.at[way, lay, rows], hal.at[k, way, lay, rows],
                    snd_sem.at[k, way, lay, c], hal_sem.at[k, way, lay, c], to,
                )))
        return out

    def send_edges(k, c):
        y = pl.multiple_of(c * WIDE, WIDE)
        rows = pl.ds(y, WIDE)
        for way, i, coef in ((0, ROWS - 1, p1), (1, 0, n1)):
            mid, out, _ = fine_row(ma, i, y, WIDE)
            mb[i + 1, pl.ds(y + PAD, WIDE), :] = out
            factor = coef[i + 1, rows, :]
            snd[way, 0, rows, :] = factor * mid
            snd[way, 1, rows, :] = factor * out
        for sends, _, copy in edge_copies(k, c):
            pl.when(sends)(copy.start)

    def take_edges(k, c):
        for _, receives, copy in edge_copies(k, c):
            pl.when(receives)(copy.wait_recv)

        y = pl.multiple_of(c * WIDE, WIDE)
        rows = pl.ds(y, WIDE)
        padded = pl.ds(y + PAD, WIDE)
        mb[1, padded, :] = mb[1, padded, :] + hal[k, 0, 0, rows, :]
        mb[ROWS, padded, :] = mb[ROWS, padded, :] + hal[k, 1, 0, rows, :]
        mb[0, padded, :] = hal[k, 0, 1, rows, :] + st[0, rows, :] * snd[1, 0, rows, :]
        mb[ROWS + 1, padded, :] = hal[k, 1, 1, rows, :] + st[1, rows, :] * snd[0, 0, rows, :]

    def edge_step(write, c):
        y = pl.multiple_of(c * WIDE, WIDE)
        for i in (0, ROWS - 1, 1, ROWS - 2):
            step_row(mb, write, i, y, WIDE)

    def wait_edges(k, c):
        for sends, _, copy in edge_copies(k, c):
            pl.when(sends)(copy.wait_send)

    def start_kinds(k):
        i = order(k + 8)
        pltpu.make_async_copy(site_class.at[i], cls.at[slot(i)], load_sem.at[3, i]).start()

    def ready(k):
        for copy in loads(order(k)):
            copy.wait()
        start_loads(k + 4)
        for n, copy in enumerate(loads(order(k + 8))):
            if n != 3:
                copy.start()

    each(4, ready)
    restrict_shifted(0, CROWS - 1)
    each(4, lambda k: fine_coefs(order(k)))
    each(4, start_kinds)

    pl.semaphore_wait(barrier, 3 + has_up.astype(jnp.int32) + has_dn.astype(jnp.int32))

    own_half = pl.ds(core * HALF, HALF)
    other_half = pl.ds((1 - core) * HALF, HALF)
    st_up = remote(p1.at[ROWS, own_half], st.at[0, own_half], st_snd.at[0], st_rcv.at[0], up)
    st_dn = remote(n1.at[1, own_half], st.at[1, own_half], st_snd.at[1], st_rcv.at[1], dn)
    pl.when(has_up)(st_up.start)
    pl.when(has_dn)(st_dn.start)

    each(CHUNKS, lambda c: send_edges(0, c))

    def more_coefs(p):
        def row(n):
            return jnp.where(n < 2, 2 * p, 2 * (CROWS - 1 - p) - 2) + n

        def arrived(n):
            for copy in loads(row(n))[:4]:
                copy.wait()

        each(4, arrived)
        restrict_shifted(p, CROWS - 1 - p)
        each(4, lambda n: fine_coefs(row(n)))

    def state_arrived(k):
        for copy in loads(order(k + 4))[4:]:
            copy.wait()

    each(ROWS - 4, state_arrived)

    inner = pl.ds(PAD, SIDE)

    def restrict_start(n):
        items = []
        for j in (2 * n, 2 * n + 1):
            items.append((lambda b, j=j: ma[2 * j + b + 1, inner, :], put(rs_own, 0, j)))
            items.append((lambda b, j=j: sv[2 * j + b], put(rs_own, 1, j)))
        restrict_pairs(items)

    each(CROWS // 2, restrict_start)

    rs_copy = remote(rs_own, rs_next, rs_sem.at[0], rs_sem.at[1], sibling)
    @pl.when(t == 1)
    def _():
        for comp in range(2):
            for j in range(CROWS):
                rs_next[comp, j] = jnp.zeros((HALF, HALF), F32)

    pl.when(t > 0)(rs_copy.start)

    fw = [remote(st.at[w, own_half], st.at[w, own_half], fw_snd.at[w], fw_rcv.at[w], sibling) for w in range(2)]
    fr = [remote(st.at[w, other_half], st.at[w, other_half], fw_snd.at[w], fw_rcv.at[w], sibling) for w in range(2)]
    def share_static():
        for w, exists, copy in ((0, has_dn, st_up), (1, has_up, st_dn)):
            @pl.when(exists)
            def _(w=w, copy=copy):
                copy.wait_recv()
                fw[w].start()
        for w, exists in ((0, has_dn), (1, has_up)):
            pl.when(exists)(fr[w].wait_recv)

    def restrict_static(j):
        restrict_pairs((
            (lambda b: p1[2 * j + b + 1] - n1[2 * j + b + 1], put(pc1, j + 1)),
            (lambda b: 2.0 * al[2 * j + b], put(alc, j)),
            (lambda b: 2.0 * be[2 * j + b], put(bec, j)),
        ))

    crow = iota((HALF, HALF), 0)
    clane = iota((HALF, HALF), 1)
    coarse_spread = 0.5 * SPREAD

    def coarse_coefs(j):
        u1, u2, u3 = pc1[j + 1], pc2[j], pc3[j]
        plus1 = jnp.maximum(u1, 0.0) + coarse_spread
        minus1 = plus1 - u1
        plus2 = jnp.maximum(u2, 0.0) + coarse_spread
        minus2 = plus2 - u2
        plus3 = jnp.maximum(u3, 0.0) + coarse_spread
        minus3 = plus3 - u3
        ccc[j] = (1.0 - (plus1 + minus1 + plus2 + minus2 + plus3 + minus3)) - alc[j]
        pc1[j + 1] = plus1
        nc1[j + 1] = minus1
        pc2[j] = jnp.where(crow == 0, 0.0, pltpu.roll(plus2, 1, 0))
        nc2[j] = jnp.where(crow == HALF - 1, 0.0, pltpu.roll(minus2, HALF - 1, 0))
        pc3[j] = jnp.where(clane == 0, 0.0, pltpu.roll(plus3, 1, 1))
        nc3[j] = jnp.where(clane == HALF - 1, 0.0, pltpu.roll(minus3, HALF - 1, 1))

    is_last = t == LAST
    runs = t % 2 == 1
    cst_up = remote(pc1.at[CROWS], cst.at[0], cst_snd.at[0], cst_rcv.at[0], up)
    cst_dn = remote(nc1.at[1], cst.at[1], cst_snd.at[1], cst_rcv.at[1], dn)

    def d_pieces(group, comp):
        if group == 0:
            return ((comp, pl.ds(2, 2)),)
        first = 2 - group
        return ((4 * group - 2 + comp, pl.ds(first, 1)), (4 * group + comp, pl.ds(CROWS - 1 - first, 1)))

    def d_copies(*groups, to=LAST):
        return [
            remote(
                d_own.at[comp, rows], dd.at[t, comp, rows],
                d_snd.at[0 if to == LAST else 1, n], d_rcv.at[t, n], {"tm": to},
            )
            for group in groups for comp in range(2) for n, rows in d_pieces(group, comp)
        ]

    def send_jump(*groups):
        for copy in d_copies(*groups):
            copy.start()

        @pl.when(t == 0)
        def _():
            for copy in d_copies(*groups, to=1):
                copy.start()

    keep = jnp.where(t == 1, 0.0, 1.0)

    def jump(*rows):
        def item(comp, j):
            def write(value):
                d_own[comp, j] = value - keep * rs_next[comp, j]
            return lambda b: ends[comp, 2 * j + b], write

        restrict_pairs([item(comp, j) for j in rows for comp in range(2)])

    def among(n, *values):
        found = n == values[0]
        for value in values[1:]:
            found = jnp.logical_or(found, n == value)
        return found

    def fill(n):
        outer = among(n, 1, 11)
        pl.when(among(n, 0, 2))(lambda: more_coefs(jnp.where(n == 0, 1, 2)))
        pl.when(outer)(lambda: (attach_edge(0), attach_edge(ROWS - 1), None)[2])

        @pl.when(among(n, 1, 3, 6, 11))
        def _():
            def body(m):
                first = jnp.where(outer, 1 + (ROWS - 4) * m, 3 + 2 * m)
                for b in range(2):
                    step_row(ma, write_b, first + b, 0, SIDE)

            each(jnp.where(outer, 2, 3), body)

        @pl.when(among(n, 4, 5))
        def _():
            each(4, lambda m: step_row(mb, write_a, 4 * n - 14 + m, 0, SIDE), unroll=2)

        @pl.when(among(n, 7, 11))
        def _():
            def body(m):
                first = jnp.where(outer, 2 + (ROWS - 6) * m, 4 + 2 * m)
                for b in range(2):
                    step_row(mb, write_end, first + b, 0, SIDE)

            each(2, body)

        @pl.when(jnp.logical_and(runs, jnp.logical_and(n >= 4, n < 10)))
        def _():
            restrict_static(n - 4)
            coarse_coefs(n - 4)

        @pl.when(jnp.logical_and(jnp.logical_not(is_last), among(n, 8, 11)))
        def _():
            pl.when(jnp.logical_and(n == 8, t != 1))(rs_copy.wait_recv)
            p = jnp.where(n == 8, 2, 1)
            jump(p, CROWS - 1 - p)
            pl.when(jnp.logical_and(n == 8, t != 1))(lambda: send_jump(0))
            pl.when(jnp.logical_and(n == 11, t != 1))(lambda: send_jump(1))

    def between(n):
        fill(n)
        pl.when(n == 1)(share_static)
        pl.when(jnp.logical_and(n >= 1, n <= CHUNKS))(lambda: take_edges(0, n - 1))
        pl.when(jnp.logical_and(n >= 2, n <= CHUNKS + 1))(lambda: edge_step(write_a, n - 2))

        @pl.when(jnp.logical_and(n >= 3, n <= CHUNKS + 2))
        def _():
            wait_edges(0, n - 3)
            send_edges(1, n - 3)

    each(CHUNKS + 4, between)

    @pl.when(runs)
    def _():
        pl.when(has_up)(cst_up.start)
        pl.when(has_dn)(cst_dn.start)
        zero = jnp.zeros((HALF, HALF), F32)
        one = jnp.ones((HALF, HALF), F32)
        pc1[0] = one
        nc1[CROWS + 1] = one
        margin = jnp.zeros((PAD, HALF), F32)
        middle = pl.ds(PAD, HALF)

        def margins(j):
            for ref in (mca, mcb):
                ref[j, pl.ds(0, PAD), :] = margin
                ref[j, pl.ds(PAD + HALF, PAD), :] = margin

        each(CROWS + 2, margins)
        for j in (0, CROWS + 1):
            mca[j, middle, :] = zero

        @pl.when(jnp.logical_not(has_dn))
        def _():
            cst[0] = zero
            for k in range(3):
                for lay in range(2):
                    chal[k, 0, lay] = zero

        @pl.when(jnp.logical_not(has_up))
        def _():
            cst[1] = zero
            for k in range(3):
                for lay in range(2):
                    chal[k, 1, lay] = zero

    def finish(n):
        pl.when(n < CHUNKS)(lambda: take_edges(1, n))
        pl.when(n >= 1)(lambda: edge_step(write_end, n - 1))

    each(CHUNKS + 1, finish)

    @pl.when(jnp.logical_not(is_last))
    def _():
        jump(0, CROWS - 1)

        @pl.when(t == 1)
        def _():
            pl.semaphore_wait(turn_sem, 1)
            for copy in d_copies(0, 1):
                copy.start()

        send_jump(2)

        @pl.when(t == 0)
        def _():
            first, second, *rest = d_copies(2)
            first.wait_send()
            second.wait_send()
            pl.semaphore_signal(turn_sem, inc=1, device_id={"tm": 1}, device_id_type=MESH)
            for copy in rest:
                copy.wait_send()

    middle = pl.ds(PAD, HALF)

    def coarse_row(src, j):
        wide = src[j + 1]
        mid = wide[PAD:PAD + HALF]
        old = sc[j]
        off = bec[j] * old
        out = ccc[j] * mid + off
        out = out + (pc1[j] * src[j, middle, :] + nc1[j + 2] * src[j + 2, middle, :])
        out = out + (pc2[j] * wide[PAD - 1:PAD - 1 + HALF] + nc2[j] * wide[PAD + 1:PAD + 1 + HALF])
        out = out + (pc3[j] * pltpu.roll(mid, 1, 1) + nc3[j] * pltpu.roll(mid, HALF - 1, 1))
        return mid, out, (old - off) + alc[j] * mid

    def coarse_second(turn, *rows):
        for j in rows:
            _, out, held = coarse_row(mcb, j)
            dd[turn - 1, 0, j] = out
            dd[turn - 1, 1, j] = held

    def coarse_edge_copies(turn):
        out = []
        for way, (to, sends, receives) in enumerate(((up, has_up, has_dn), (dn, has_dn, has_up))):
            for lay in range(2):
                out.append((sends, receives, remote(
                    csnd.at[way, lay], chal.at[turn - 1, way, lay],
                    c_snd.at[turn - 1, way, lay], c_rcv.at[turn - 1, way, lay], to,
                )))
        return out

    g_copy = remote(dd.at[1], g_in, g_sem.at[0], g_sem.at[1], {"tm": 2})

    def chain(turn):
        for group, comp in ((0, 0), (0, 1), (1, 0), (1, 1), (2, 0), (2, 1)):
            for n, rows in d_pieces(group, comp):
                remote(
                    d_own.at[comp, rows], dd.at[turn - 1, comp, rows],
                    d_snd.at[0, n], d_rcv.at[turn - 1, n], {"tm": 0},
                ).wait_recv()

        taken = jnp.where(turn == 2, 1.0, 0.0)
        pl.when(turn == 2)(rs_copy.wait_recv)

        @pl.when(turn == 1)
        def _():
            for j in range(CROWS):
                mca[j + 1, middle, :] = dd[0, 0, j]
                sc[j] = dd[0, 1, j]

        @pl.when(turn > 1)
        def _():
            for j in range(CROWS):
                mca[j + 1, middle, :] = (dd[turn - 1, 0, j] - taken * rs_next[0, j]) + dd[turn - 2, 0, j]
                sc[j] = (dd[turn - 1, 1, j] - taken * rs_next[1, j]) + dd[turn - 2, 1, j]

        @pl.when(turn > 1)
        def _():
            for sends, _, copy in coarse_edge_copies(turn - 1):
                pl.when(sends)(copy.wait_send)

        for way, j, coef in ((0, CROWS - 1, pc1), (1, 0, nc1)):
            mid, out, _ = coarse_row(mca, j)
            mcb[j + 1, middle, :] = out
            factor = coef[j + 1]
            csnd[way, 0] = factor * mid
            csnd[way, 1] = factor * out
        for sends, _, copy in coarse_edge_copies(turn):
            pl.when(sends)(copy.start)

        for j in (0, CROWS - 1):
            old = sc[j]
            sc[j] = (old - bec[j] * old) + alc[j] * mca[j + 1, middle, :]
        for j in range(1, CROWS - 1):
            _, out, held = coarse_row(mca, j)
            mcb[j + 1, middle, :] = out
            sc[j] = held
        coarse_second(turn, *range(2, CROWS - 2))

        @pl.when(turn == 1)
        def _():
            pl.when(has_dn)(cst_up.wait_recv)
            pl.when(has_up)(cst_dn.wait_recv)

        for _, receives, copy in coarse_edge_copies(turn):
            pl.when(receives)(copy.wait_recv)
        mcb[1, middle, :] = mcb[1, middle, :] + chal[turn - 1, 0, 0]
        mcb[CROWS, middle, :] = mcb[CROWS, middle, :] + chal[turn - 1, 1, 0]
        mcb[0, middle, :] = chal[turn - 1, 0, 1] + cst[0] * csnd[1, 0]
        mcb[CROWS + 1, middle, :] = chal[turn - 1, 1, 1] + cst[1] * csnd[0, 0]
        coarse_second(turn, 0, CROWS - 1, 1, CROWS - 2)

        pl.when(turn == 2)(g_copy.start)

    @pl.when(runs)
    def _():
        turns = jnp.where(is_last, LAST, 1)
        each(turns, lambda n: chain(n + 1))

        def result(j):
            g_out[0, j] = dd[turns - 1, 0, j]
            g_out[1, j] = dd[turns - 1, 1, j]

        each(CROWS, result, unroll=CROWS)
        pl.when(is_last)(g_copy.wait_send)
        for sends, _, copy in coarse_edge_copies(turns):
            pl.when(sends)(copy.wait_send)
        pl.when(has_up)(cst_up.wait_send)
        pl.when(has_dn)(cst_dn.wait_send)

    @pl.when(t == 2)
    def _():
        g_copy.wait_recv()

        def result(j):
            g_out[0, j] = g_in[0, j]
            g_out[1, j] = g_in[1, j]

        each(CROWS, result, unroll=CROWS)

    @pl.when(t == 0)
    def _():
        def result(j):
            g_out[0, j] = jnp.zeros((HALF, HALF), F32)
            g_out[1, j] = jnp.zeros((HALF, HALF), F32)

        each(CROWS, result, unroll=CROWS)
        for copy in d_copies(0, 1) + d_copies(0, 1, 2, to=1):
            copy.wait_send()

    @pl.when(jnp.logical_or(t == 1, t == 2))
    def _():
        for copy in d_copies(0, 1, 2):
            copy.wait_send()

    each(CHUNKS, lambda c: wait_edges(1, c))
    pl.when(has_up)(st_up.wait_send)
    pl.when(has_dn)(st_dn.wait_send)
    pl.when(has_dn)(fw[0].wait_send)
    pl.when(has_up)(fw[1].wait_send)
    pl.when(t > 0)(rs_copy.wait_send)


def final_kernel(ends, g, out, buf, sem):
    wide = (iota((HALF, SIDE), 0) == (iota((HALF, SIDE), 1) // 2)).astype(F32).astype(BF16)
    tall = ((iota((SIDE, HALF), 0) // 2) == iota((SIDE, HALF), 1)).astype(F32).astype(BF16)

    def copy(comp, i):
        return pltpu.make_async_copy(buf.at[comp, i], out.at[comp, i], sem.at[comp, i])

    def body(n):
        comp, j = n // CROWS, n % CROWS
        spread = None
        for part in split(g[comp, j]):
            term = dot(tall, dot(part, wide).astype(BF16))
            spread = term if spread is None else spread + term
        for b in range(2):
            buf[comp, 2 * j + b] = ends[comp, 2 * j + b] + spread
            copy(comp, 2 * j + b).start()

    each(2 * CROWS, body, unroll=6)
    each(2 * ROWS, lambda n: copy(n // ROWS, n % ROWS).wait())


def per_device(start_states, velocity, site_class, attach_rates, detach_rates):
    any_ref = pl.BlockSpec(memory_space=pl.ANY)
    smem = pl.BlockSpec(memory_space=pltpu.SMEM)
    vmem = pl.BlockSpec(memory_space=pltpu.VMEM)
    start = start_states.reshape(start_states.shape[1:])
    plane = (SIDE, SIDE)
    cplane = (HALF, HALF)
    coarse = (2, CROWS) + cplane

    def buf(*shape):
        return pltpu.VMEM(shape, F32)

    brick = buf(ROWS, *plane)
    cbrick = buf(CROWS, *cplane)
    dma = pltpu.SemaphoreType.DMA
    ends, g = pl.pallas_call(
        main_kernel,
        out_shape=(pltpu.VMEM((2, ROWS) + plane, F32), pltpu.VMEM(coarse, F32)),
        in_specs=[any_ref, any_ref, any_ref, smem, smem],
        out_specs=(vmem, vmem),
        scratch_shapes=[
            buf(ROWS + 2, SIDE + 2 * PAD, SIDE), buf(ROWS + 2, SIDE + 2 * PAD, SIDE),
            buf(ROWS + 2, *plane), buf(ROWS + 2, *plane), brick, brick, brick, brick, brick, brick, brick,
            pltpu.VMEM((8,) + plane, jnp.int32),
            buf(2, 2, *plane), buf(2, 2, 2, *plane), buf(2, *plane),
            buf(*coarse), buf(*coarse), buf(*coarse), buf(3, *coarse), buf(*coarse),
            buf(CROWS + 2, HALF + 2 * PAD, HALF), buf(CROWS + 2, HALF + 2 * PAD, HALF), cbrick,
            buf(CROWS + 2, *cplane), buf(CROWS + 2, *cplane), cbrick, cbrick, cbrick, cbrick, cbrick, cbrick, cbrick,
            buf(2, 2, *cplane), buf(3, 2, 2, *cplane), buf(2, *cplane), buf(PLANES, SIDE, HALF),
            dma((6, ROWS)), dma((2, 2, 2, CHUNKS)), dma((2, 2, 2, CHUNKS)), dma((2,)), dma((2,)), dma((2,)), dma((2,)),
            dma((2,)), pltpu.SemaphoreType.REGULAR, dma((2, 10)), dma((3, 10)), dma((2,)), dma((3, 2, 2)), dma((3, 2, 2)), dma((2,)), dma((2,)),
        ],
        compiler_params=pltpu.CompilerParams(
            collective_id=0, has_side_effects=True, vmem_limit_bytes=56 * 1024 * 1024
        ),
    )(start, velocity, site_class, attach_rates, detach_rates)
    out = pl.pallas_call(
        final_kernel,
        out_shape=jax.ShapeDtypeStruct((2, ROWS) + plane, F32),
        in_specs=[vmem, vmem],
        out_specs=any_ref,
        scratch_shapes=[buf(2, ROWS, *plane), dma((2, ROWS))],
        compiler_params=pltpu.CompilerParams(vmem_limit_bytes=40 * 1024 * 1024),
    )(ends, g)
    return out[None]


def solution(mesh):
    in_specs = (
        P("tm", None, "space", None, None),
        P(None, "space", None, None),
        P("space", None, None),
        P(),
        P(),
    )
    return jax.shard_map(
        per_device, mesh=mesh, in_specs=in_specs, out_specs=P("tm", None, "space", None, None), check_vma=False
    )
```
